128 devices in a mesh: member: 8 (over x_hi, z), space: 8 (over y, core), dp: 2 (over x_lo).
Axes of the slice: x: 4 (x_hi: 2, x_lo: 2; x = x_hi * 2 + x_lo), y: 4, z: 4, core: 2. Of those that a mesh axis runs over, the one named last changes fastest.
Arguments:
- latent: bfloat16 [2, 16, 16384, 1024], P('dp', 'member', 'space'), may hold values from -6 to 6
- w_in: bfloat16 [1024, 1024], replicated, may hold values from -0.1875 to 0.1875
- w_out: bfloat16 [1024, 100], replicated, may hold values from -0.1875 to 0.1875
- targets: bfloat16 [2, 100, 16384], P('dp', None, 'space'), may hold values from -4 to 4
- area_units: int32 [16384], P('space'), may hold values from 1000 to 3499
- var_weight: float32 [100], replicated, may hold values from 0.3 to 3
Outputs:
- loss: float32 [], replicated
- grad_latent: bfloat16 [2, 16, 16384, 1024], P('dp', 'member', 'space')
- grad_w_in: float32 [1024, 1024], P(('member', 'space', 'dp'))
- grad_w_out: float32 [1024, 100], P(('member', 'space', 'dp'))
The draws below stay inside these ranges and needn't reach their ends.
All inputs are finite; a program needn't handle non-finite values.
Results may differ from the reference program's by a relative error of at most 0.025.
Values may be sent and summed in bfloat16 or wider, within the bound.
No kernel may reach another device: no remote copies, remote signals or barrier semaphores. Data moves between devices by JAX's collectives and lax.ppermute only.
A program may use at most 192 MiB of HBM per device.

```python
import math
import jax
import jax.numpy as jnp
from jax import lax

HID = 1024
V = 100
PTS_DEV = 2048
MEMBERS = 16
NPOINTS = 16384
DATES = 2


def draw_area_units(key, part):
    key = jax.random.fold_in(key, 7)
    subkeys = jax.random.split(key, 6)
    rise_span = jax.random.randint(subkeys[0], (), 1000, 2001)
    base_level = jax.random.randint(subkeys[1], (), 0, 2001 - rise_span)
    positions = jnp.arange(NPOINTS, dtype=jnp.int32)
    blocks = NPOINTS // PTS_DEV
    block_steps = jax.random.randint(subkeys[2], (blocks,), 0, 250)
    block_step = block_steps[positions // PTS_DEV]
    jitter = jax.random.randint(subkeys[3], (NPOINTS,), 0, 250)
    area_values = 1000 + base_level + rise_span * positions // NPOINTS + block_step + jitter
    low_at = jax.random.randint(subkeys[4], (), 0, NPOINTS)
    high_at = (low_at + 1 + jax.random.randint(subkeys[5], (), 0, NPOINTS - 1)) % NPOINTS
    area_values = area_values.at[low_at].set(1000).at[high_at].set(3499)
    return area_values.astype(jnp.int32)


def spiked(result, rng, source, target, parts, factor):
    def block_of(axis_at):
        return (jnp.arange(result.shape[axis_at]) // (result.shape[axis_at] // parts)).reshape((-1,) + (1,) * (result.ndim - 1 - axis_at))

    one_side = jax.random.permutation(rng, parts)[block_of(target)]
    second = (block_of(target) + parts // 2) % parts
    return jnp.where((block_of(source) == one_side) | (block_of(source) == second), factor * result, result)


def shard_levels(key, shape, shards, least, largest):
    def one(axis_at, blocks):
        steps = jax.random.uniform(jax.random.fold_in(jax.random.fold_in(key, 6), axis_at), (blocks,), jnp.float32, least / len(shards), largest / len(shards))
        return jnp.repeat(jnp.exp(steps), shape[axis_at] // blocks).reshape((-1,) + (1,) * (len(shape) - axis_at - 1))

    gain = one(*shards[0])
    for cut in shards[1:]:
        gain = gain * one(*cut)
    return gain


def normal_values(own_key, shape, deviation, most, cuts=(), kind=jnp.bfloat16):
    entries = jax.random.normal(own_key, shape, jnp.float32) * deviation
    if len(cuts) > 0:
        entries = shard_levels(own_key, shape, cuts, -0.22, 0.18) * entries
    return jnp.clip(entries, min=-most, max=most).astype(kind)


def noise_with(rng, extent, deviation, reach, shards, heavy, kind=jnp.bfloat16):
    drawn = deviation * jax.random.normal(rng, extent, jnp.float32)
    if shards:
        drawn = drawn * shard_levels(rng, extent, shards, -0.22, 0.18)
    return jnp.clip(spiked(drawn, jax.random.fold_in(rng, 3), *heavy), -reach, reach).astype(kind)


def setup_inputs(seed: int = 0) -> dict:
    seeds = jax.random.split(jax.random.key(seed), 7)
    latent = noise_with(seeds[0], (DATES, MEMBERS, NPOINTS, HID), 1.0, 6.0, ((0, 2), (1, 8), (2, 8)), (2, 3, 8, 2.0))
    w_in = normal_values(seeds[1], (HID, HID), HID ** -0.5, 0.1875)
    w_out = normal_values(seeds[2], (HID, V), HID ** -0.5, 0.1875)
    targets = normal_values(seeds[3], (DATES, V, NPOINTS), 0.5, 4.0, ((0, 2), (2, 8)))
    area_units = draw_area_units(jax.random.fold_in(seeds[6], 71), 0)
    var_weight = jnp.clip(jnp.exp(jax.random.uniform(seeds[5], (V,), jnp.float32, math.log(0.3), math.log(3.0))), 0.3, 3.0)
    return {"latent": latent, "w_in": w_in, "w_out": w_out, "targets": targets, "area_units": area_units, "var_weight": var_weight}


GELU_C = 0.7978845608
SMOOTH = 0.01

def gelu_parts(preact):
    inner = GELU_C * (preact + 0.044715 * preact * preact * preact)
    tangent = jnp.tanh(inner)
    value = 0.5 * preact * (1.0 + tangent)
    slopes = 0.5 * (1.0 + tangent) + 0.5 * preact * (1.0 - tangent * tangent) * GELU_C * (1.0 + 3.0 * 0.044715 * preact * preact)
    return (value, slopes)

def reference(latent, w_in, w_out, targets, area_units, var_weight):
    row_blocks = latent.reshape(DATES * MEMBERS, NPOINTS, HID)

    def forward(block):
        preact = jnp.dot(block, w_in, preferred_element_type=jnp.float32)
        value, slopes = gelu_parts(preact)
        hidden = value.astype(jnp.bfloat16)
        return lax.dot_general(w_out, hidden, (((0,), (1,)), ((), ())), preferred_element_type=jnp.float32).astype(jnp.bfloat16)
    pred = lax.map(forward, row_blocks).reshape(DATES, MEMBERS, V, NPOINTS)
    area = area_units.astype(jnp.float32)
    area_norm = area * NPOINTS / jnp.sum(area)
    weight = var_weight[:, None] * area_norm[None, :]
    values = pred.astype(jnp.float32)
    truth = targets.astype(jnp.float32)
    to_truth = values - truth[:, None]
    phi_truth = jnp.sqrt(to_truth * to_truth + SMOOTH)

    def pair_sums(member_values):
        spread = member_values[:, None] - values
        phi_pair = jnp.sqrt(spread * spread + SMOOTH)
        return (lax.optimization_barrier(jnp.sum(phi_pair, axis=1)), lax.optimization_barrier(jnp.sum(spread / phi_pair, axis=1)))
    pair_phi, pair_grad = lax.map(pair_sums, jnp.moveaxis(values, 1, 0))
    pair_phi = jnp.moveaxis(pair_phi, 0, 1)
    pair_grad = jnp.moveaxis(pair_grad, 0, 1)
    share = phi_truth - pair_phi / (2.0 * (MEMBERS - 1))
    loss = jnp.sum(weight * share) / (DATES * NPOINTS * V)
    grad_pred = (weight * (to_truth / phi_truth - pair_grad / (MEMBERS - 1))).astype(jnp.bfloat16)
    grad_rows = grad_pred.reshape(DATES * MEMBERS, V, NPOINTS)

    def backward(carry, items):
        block, upstream = items
        preact = jnp.dot(block, w_in, preferred_element_type=jnp.float32)
        value, slopes = gelu_parts(preact)
        hidden = value.astype(jnp.bfloat16)
        grad_hidden = lax.dot_general(upstream, w_out, (((0,), (1,)), ((), ())), preferred_element_type=jnp.float32)
        grad_preact = (grad_hidden * slopes).astype(jnp.bfloat16)
        grad_block = jnp.dot(grad_preact, w_in.T, preferred_element_type=jnp.float32).astype(jnp.bfloat16)
        sum_in = carry[0] + jnp.dot(block.T, grad_preact, preferred_element_type=jnp.float32)
        sum_out = carry[1] + jnp.dot(hidden.T, upstream.T, preferred_element_type=jnp.float32)
        return ((sum_in, sum_out), grad_block)
    start = (jnp.zeros((HID, HID), jnp.float32), jnp.zeros((HID, V), jnp.float32))
    (sum_in, sum_out), grad_blocks = lax.scan(backward, start, (row_blocks, grad_rows))
    grad_scale = math.sqrt(DATES * MEMBERS * NPOINTS)
    grad_latent = grad_blocks.reshape(DATES, MEMBERS, NPOINTS, HID)
    return (loss, grad_latent, sum_in / grad_scale, sum_out / grad_scale)
```

```python
import functools
import math

import jax
import jax.numpy as jnp
from jax import lax
from jax.experimental import pallas as pl
from jax.experimental.pallas import tpu as pltpu
from jax.sharding import Mesh
from jax.sharding import PartitionSpec as P

GELU_C = 0.7978845608
GELU_A = 0.044715
SMOOTH = 0.01
BF16 = jnp.bfloat16
F32 = jnp.float32

BLOCK = 256
VPAD = 112
WIDE = 128
TILE = 512
SUB = 256
EXTRA = 112

MEMBER = ("xh", "z")
REST = ("xh", "z", "y", "dp")


def forward_kernel(lat_ref, win_ref, wout_ref, hidden_ref, slope_ref, pred_ref):
    for s in range(TILE // SUB):
        rows = pl.ds(s * SUB, SUB)
        u = jnp.dot(lat_ref[0, rows, :], win_ref[...], preferred_element_type=F32)
        u2 = u * u
        half = 0.5 + 0.5 * jnp.tanh(u * (GELU_C + (GELU_C * GELU_A) * u2))
        value = u * half
        hidden = value.astype(BF16)
        hidden_ref[0, rows, :] = hidden
        bend = (2.0 * GELU_C) + (6.0 * GELU_A * GELU_C) * u2
        slope_ref[0, rows, :] = (half + (value - value * half) * bend).astype(BF16)
        pred = jnp.dot(hidden, wout_ref[...], preferred_element_type=F32)
        pred_ref[s, 0] = pred.T[:VPAD].astype(BF16)


def forward(latent, w_in, w_out):
    members, points, channels = latent.shape
    per = TILE // BLOCK
    tile = pl.BlockSpec((1, TILE, channels), lambda m, i: (m, i, 0))
    return pl.pallas_call(
        forward_kernel,
        grid=(members, points // TILE),
        in_specs=[
            tile,
            pl.BlockSpec((channels, channels), lambda m, i: (0, 0)),
            pl.BlockSpec((channels, WIDE), lambda m, i: (0, 0)),
        ],
        out_specs=[
            tile,
            tile,
            pl.BlockSpec((per, 1, VPAD, BLOCK), lambda m, i: (i, m, 0, 0)),
        ],
        out_shape=[
            jax.ShapeDtypeStruct(latent.shape, BF16),
            jax.ShapeDtypeStruct(latent.shape, BF16),
            jax.ShapeDtypeStruct((points // BLOCK, members, VPAD, BLOCK), BF16),
        ],
        compiler_params=pltpu.CompilerParams(vmem_limit_bytes=40 << 20),
        name="forward",
    )(latent, w_in, w_out)


def score_kernel(members, scale_ref, pred_ref, truth_ref, var_ref, area_ref, grad_ref, share_ref):
    per = pred_ref.shape[1]
    scale = scale_ref[0, 0]
    self_phi = members * math.sqrt(SMOOTH) / (2.0 * (members - 1))

    def rows16(step, total):
        base = pl.multiple_of(step * 16, 16)
        rows = pl.ds(base, 16)
        for lane in range(BLOCK // 128):
            lanes = pl.ds(lane * 128, 128)
            loaded = [pred_ref[m // per, m % per, rows, lanes].astype(F32) for m in range(members)]
            truths = truth_ref[rows, lanes].astype(F32)
            area = area_ref[0, :, lanes].astype(F32) * scale
            weights = var_ref[rows, lanes] * area
            results = []
            for h in range(2):
                x = [v[h * 8 : h * 8 + 8] for v in loaded]
                truth = truths[h * 8 : h * 8 + 8]
                weight = weights[h * 8 : h * 8 + 8]
                grads = [None] * members
                pair_phi = None
                for m in range(members):
                    for k in range(m + 1, members):
                        d = x[m] - x[k]
                        q = d * d + SMOOTH
                        r = lax.rsqrt(q)
                        g = d * r
                        p = q * r
                        pair_phi = p if pair_phi is None else pair_phi + p
                        grads[m] = g if grads[m] is None else grads[m] + g
                        grads[k] = -g if grads[k] is None else grads[k] - g
                truth_phi = None
                outs = []
                for m in range(members):
                    d = x[m] - truth
                    q = d * d + SMOOTH
                    r = lax.rsqrt(q)
                    p = q * r
                    truth_phi = p if truth_phi is None else truth_phi + p
                    outs.append(weight * (d * r - grads[m] * (1.0 / (members - 1))))
                total = total + weight * (truth_phi - pair_phi * (1.0 / (members - 1)) - self_phi)
                results.append(outs)
            for m in range(members):
                grad_ref[m // per, m % per, rows, lanes] = jnp.concatenate(
                    [results[0][m], results[1][m]], axis=0
                ).astype(BF16)
        return total

    share_ref[...] = lax.fori_loop(0, VPAD // 16, rows16, jnp.zeros((8, 128), F32))


def score(me, scale, every, truth, var_weight, area):
    devices, per = every.shape[:2]
    members = devices * per
    grid_spec = pltpu.PrefetchScalarGridSpec(
        num_scalar_prefetch=1,
        grid=(1,),
        in_specs=[
            pl.BlockSpec(memory_space=pltpu.SMEM),
            pl.BlockSpec(every.shape, lambda i, me: (0, 0, 0, 0)),
            pl.BlockSpec((VPAD, BLOCK), lambda i, me: (0, me[0])),
            pl.BlockSpec((VPAD, BLOCK), lambda i, me: (0, 0)),
            pl.BlockSpec((1, 1, BLOCK), lambda i, me: (me[0], 0, 0)),
        ],
        out_specs=[
            pl.BlockSpec(every.shape, lambda i, me: (0, 0, 0, 0)),
            pl.BlockSpec((8, 128), lambda i, me: (0, 0)),
        ],
    )

    def kernel(me_ref, *refs):
        score_kernel(members, *refs)

    return pl.pallas_call(
        kernel,
        grid_spec=grid_spec,
        out_shape=[
            jax.ShapeDtypeStruct(every.shape, BF16),
            jax.ShapeDtypeStruct((8, 128), F32),
        ],
        compiler_params=pltpu.CompilerParams(vmem_limit_bytes=32 << 20),
        name="score",
    )(me, scale, every, truth, var_weight, area)


def backward_kernel(
    core_ref, lat_ref, hidden_ref, slope_ref, up_ref, wout_ref, share_ref, gp_ref, sums_ref, acc_in, acc_out
):
    step, last = pl.program_id(0), pl.num_programs(0) - 1
    channels = lat_ref.shape[2]

    @pl.when(step == 0)
    def _():
        acc_in[...] = jnp.zeros_like(acc_in)
        acc_out[...] = jnp.zeros_like(acc_out)

    ups = []
    for s in range(TILE // BLOCK):
        rows = pl.ds(s * BLOCK, BLOCK)
        block = jnp.concatenate(
            [up_ref[s, 0].astype(F32), jnp.zeros((WIDE - VPAD, BLOCK), F32)], axis=0
        )
        up = block.T.astype(BF16)
        ups.append(up)
        grad_hidden = jnp.dot(up, wout_ref[...], preferred_element_type=F32)
        gp_ref[0, rows, :] = (grad_hidden * slope_ref[0, rows, :].astype(F32)).astype(BF16)
    over_rows = (((0,), (0,)), ((), ()))
    acc_in[...] += lax.dot_general(
        lat_ref[0], gp_ref[0], over_rows, preferred_element_type=F32
    )
    acc_out[...] += lax.dot_general(
        hidden_ref[0], jnp.concatenate(ups, axis=0), over_rows, preferred_element_type=F32
    )

    @pl.when(step == last)
    def _():
        sums_ref[:, :channels] = acc_in[...].astype(BF16)
        share = jnp.sum(share_ref[...])
        high = share.astype(BF16).astype(F32)
        middle = (share - high).astype(BF16).astype(F32)
        low = share - high - middle
        column = lax.broadcasted_iota(jnp.int32, acc_out.shape, 1) - (EXTRA + 3 * core_ref[0])
        sums_ref[:, channels:] = jnp.where(
            column == 0,
            high,
            jnp.where(column == 1, middle, jnp.where(column == 2, low, acc_out[...])),
        ).astype(BF16)


def backward(core, latent, hidden, slopes, upstream, w_out_t, share):
    members, points, channels = latent.shape
    steps = points // TILE
    per = TILE // BLOCK
    tile = pl.BlockSpec((1, TILE, channels), lambda i, c: (i // steps, i % steps, 0))
    grid_spec = pltpu.PrefetchScalarGridSpec(
        num_scalar_prefetch=1,
        grid=(members * steps,),
        in_specs=[
            tile,
            tile,
            tile,
            pl.BlockSpec((per, 1, VPAD, BLOCK), lambda i, c: (i % steps, i // steps, 0, 0)),
            pl.BlockSpec((WIDE, channels), lambda i, c: (0, 0)),
            pl.BlockSpec((8, 128), lambda i, c: (0, 0)),
        ],
        out_specs=[
            tile,
            pl.BlockSpec((channels, channels + WIDE), lambda i, c: (0, 0)),
        ],
        scratch_shapes=[
            pltpu.VMEM((channels, channels), F32),
            pltpu.VMEM((channels, WIDE), F32),
        ],
    )
    return pl.pallas_call(
        backward_kernel,
        grid_spec=grid_spec,
        out_shape=[
            jax.ShapeDtypeStruct(latent.shape, BF16),
            jax.ShapeDtypeStruct((channels, channels + WIDE), BF16),
        ],
        compiler_params=pltpu.CompilerParams(vmem_limit_bytes=48 << 20),
        name="backward",
    )(core, latent, hidden, slopes, upstream, w_out_t, share)


def latent_kernel(gp_ref, win_ref, out_ref):
    for s in range(TILE // SUB):
        rows = pl.ds(s * SUB, SUB)
        out_ref[0, rows, :] = lax.dot_general(
            gp_ref[0, rows, :], win_ref[...], (((1,), (1,)), ((), ())), preferred_element_type=F32
        ).astype(BF16)


def latent_grad(gp, w_in):
    members, points, channels = gp.shape
    tile = pl.BlockSpec((1, TILE, channels), lambda m, i: (m, i, 0))
    return pl.pallas_call(
        latent_kernel,
        grid=(members, points // TILE),
        in_specs=[tile, pl.BlockSpec((channels, channels), lambda m, i: (0, 0))],
        out_specs=tile,
        out_shape=jax.ShapeDtypeStruct(gp.shape, BF16),
        compiler_params=pltpu.CompilerParams(vmem_limit_bytes=24 << 20),
        cost_estimate=pl.CostEstimate(
            flops=2 * members * points * channels * channels,
            bytes_accessed=4 * members * points * channels,
            transcendentals=0,
        ),
        name="latent_grad",
    )(gp, w_in)


def exchange(x, axis, xor):
    size = lax.axis_size(axis)
    return lax.ppermute(x, axis, [(i, i ^ xor) for i in range(size)])


def body(latent, w_in, w_out, targets, area_units, var_weight):
    date_count, per, points, channels = latent.shape
    variables = w_out.shape[1]
    member_devices = lax.axis_size("xh") * lax.axis_size("z")
    members = per * member_devices
    npoints = points * lax.axis_size("y") * lax.axis_size("core")
    dates = date_count * lax.axis_size("dp")
    me = (lax.axis_index("xh") * lax.axis_size("z") + lax.axis_index("z")).astype(jnp.int32)
    core = lax.axis_index("core").astype(jnp.int32)

    area_total = jnp.sum(area_units.astype(F32))
    for axis, xor in (("core", 1), ("y", 1), ("y", 2)):
        area_total = area_total + exchange(area_total, axis, xor)
    scale = (npoints / area_total).reshape(1, 1)

    rows = latent.reshape(date_count * per, points, channels)
    w_out_wide = jnp.pad(w_out, ((0, 0), (0, WIDE - variables)))
    hidden, slopes, pred = forward(rows, w_in, w_out_wide)
    every = lax.all_to_all(pred, MEMBER, 0, 0, tiled=True)
    truth = jnp.pad(targets[0], ((0, VPAD - variables), (0, 0)))
    var_wide = jnp.broadcast_to(
        jnp.pad(var_weight, (0, VPAD - variables))[:, None], (VPAD, BLOCK)
    )
    area = area_units.reshape(points // BLOCK, 1, BLOCK)
    grad_pred, share = score(me.reshape(1), scale, every, truth, var_wide, area)
    upstream = lax.all_to_all(grad_pred, MEMBER, 0, 0, tiled=True)
    gp, sums = backward(core.reshape(1), rows, hidden, slopes, upstream, w_out_wide.T, share)
    wide = channels + WIDE
    halves = sums.reshape(-1, 2, 16, wide)
    mine = lax.dynamic_index_in_dim(halves, core, 1, keepdims=False)
    other = lax.dynamic_index_in_dim(halves, 1 - core, 1, keepdims=False)
    both = (mine.astype(F32) + exchange(other, "core", 1).astype(F32)).astype(BF16)
    pieces = lax.all_to_all(both.reshape(-1, 8, wide), REST, 0, 0, tiled=True)
    grad_latent = latent_grad(gp, w_in)
    total = jnp.sum(pieces.astype(F32), axis=0)
    grad_scale = math.sqrt(dates * members * npoints)
    loss = jnp.sum(total[0, channels + EXTRA : channels + EXTRA + 6]) / (dates * npoints * variables)
    return (
        loss,
        grad_latent.reshape(latent.shape),
        total[:, :channels] / grad_scale,
        total[:, channels : channels + variables] / grad_scale,
    )


def solution(mesh):
    fine = Mesh(mesh.devices.reshape(2, 4, 4, 2, 2), ("xh", "z", "y", "core", "dp"))
    return jax.shard_map(
        body,
        mesh=fine,
        in_specs=(
            P("dp", MEMBER, ("y", "core"), None),
            P(),
            P(),
            P("dp", None, ("y", "core")),
            P(("y", "core")),
            P(),
        ),
        out_specs=(
            P(),
            P("dp", MEMBER, ("y", "core"), None),
            P(("xh", "z", "y", "core", "dp"), None),
            P(("xh", "z", "y", "core", "dp"), None),
        ),
        check_vma=False,
    )
```

```python
import functools
import math

import jax
import jax.numpy as jnp
from jax import lax
from jax.experimental import pallas as pl
from jax.experimental.pallas import tpu as pltpu
from jax.sharding import Mesh
from jax.sharding import PartitionSpec as P

GELU_C = 0.7978845608
GELU_A = 0.044715
SMOOTH = 0.01
BF16 = jnp.bfloat16
F32 = jnp.float32

BLOCK = 256
VPAD = 112
WIDE = 128
TILE = 512
SUB = 256
EXTRA = 112

FORWARD_VMEM = 20 << 20
SHAPE_VMEM = 12 << 20
SCORE_VMEM = 8 << 20
BACKWARD_VMEM = 28 << 20
LATENT_VMEM = 16 << 20

MEMBER = ("xh", "z")
REST = ("xh", "z", "y", "dp")


def in_hbm(x):
    return pltpu.with_memory_space_constraint(x, pltpu.HBM)


def widen(wide_ref, wout_ref):
    variables = wout_ref.shape[0]
    wide_ref[...] = jnp.zeros_like(wide_ref)
    wide_ref[:variables, :] = wout_ref[...]


def forward_kernel(lat_ref, win_ref, wout_ref, preact_ref, pred_ref, wide_ref):
    @pl.when((pl.program_id(0) == 0) & (pl.program_id(1) == 0))
    def _():
        widen(wide_ref, wout_ref)

    for s in range(TILE // SUB):
        rows = pl.ds(s * SUB, SUB)
        u = jnp.dot(lat_ref[0, rows, :], win_ref[...], preferred_element_type=F32).astype(BF16)
        preact_ref[0, rows, :] = u
        bent = jnp.tanh(u * (BF16(GELU_C) + BF16(GELU_C * GELU_A) * (u * u)))
        twice = u + u * bent
        pred = lax.dot_general(
            twice, wide_ref[...], (((1,), (1,)), ((), ())), preferred_element_type=F32
        )
        pred_ref[s, 0] = (0.5 * pred.T[:VPAD]).astype(BF16)


def forward(latent, w_in, w_out_t):
    members, points, channels = latent.shape
    per = TILE // BLOCK
    tile = pl.BlockSpec((1, TILE, channels), lambda m, i: (m, i, 0))
    return pl.pallas_call(
        forward_kernel,
        grid=(members, points // TILE),
        in_specs=[
            tile,
            pl.BlockSpec((channels, channels), lambda m, i: (0, 0)),
            pl.BlockSpec(w_out_t.shape, lambda m, i: (0, 0)),
        ],
        out_specs=[
            tile,
            pl.BlockSpec((per, 1, VPAD, BLOCK), lambda m, i: (i, m, 0, 0)),
        ],
        out_shape=[
            pltpu.HBM(latent.shape, BF16),
            jax.ShapeDtypeStruct((points // BLOCK, members, VPAD, BLOCK), BF16),
        ],
        scratch_shapes=[pltpu.VMEM((WIDE, channels), BF16)],
        compiler_params=pltpu.CompilerParams(vmem_limit_bytes=FORWARD_VMEM),
        name="forward",
    )(in_hbm(latent), in_hbm(w_in), w_out_t)


def shape_kernel(preact_ref, hidden_ref, slope_ref):
    u = preact_ref[...].astype(F32)
    u2 = u * u
    half = 0.5 + 0.5 * jnp.tanh(u * (GELU_C + (GELU_C * GELU_A) * u2))
    value = u * half
    hidden_ref[...] = value.astype(BF16)
    bend = (2.0 * GELU_C) + (6.0 * GELU_A * GELU_C) * u2
    slope_ref[...] = (half + (value - value * half) * bend).astype(BF16)


def shape(preact):
    members, points, channels = preact.shape
    tile = pl.BlockSpec((1, TILE, channels), lambda m, i: (m, i, 0))
    return pl.pallas_call(
        shape_kernel,
        grid=(members, points // TILE),
        in_specs=[tile],
        out_specs=[tile, tile],
        out_shape=[pltpu.HBM(preact.shape, BF16)] * 2,
        compiler_params=pltpu.CompilerParams(vmem_limit_bytes=SHAPE_VMEM),
        cost_estimate=pl.CostEstimate(
            flops=16 * preact.size, bytes_accessed=6 * preact.size, transcendentals=preact.size
        ),
        name="shape",
    )(in_hbm(preact))


def score_kernel(members, scale_ref, pred_ref, truth_ref, var_ref, area_ref, grad_ref, share_ref):
    per = pred_ref.shape[1]
    scale = scale_ref[0, 0]
    self_phi = members * math.sqrt(SMOOTH) / (2.0 * (members - 1))

    smooth = BF16(SMOOTH)

    def parts(d):
        q = d * d + smooth
        r = lax.rsqrt(q)
        return q * r, d * r

    def rows16(step, total):
        rows = pl.ds(pl.multiple_of(step * 16, 16), 16)
        for lane in range(BLOCK // 128):
            lanes = pl.ds(lane * 128, 128)
            x = [pred_ref[m // per, m % per, rows, lanes] for m in range(members)]
            truth = truth_ref[rows, lanes]
            weight = var_ref[rows, lanes] * (area_ref[0, :, lanes].astype(F32) * scale)
            grads = [None] * members
            pair_phi = jnp.zeros((16, 128), F32)
            for m in range(members - 1):
                row_phi = None
                for k in range(m + 1, members):
                    p, g = parts(x[m] - x[k])
                    row_phi = p if row_phi is None else row_phi + p
                    grads[m] = g if grads[m] is None else grads[m] + g
                    grads[k] = -g if grads[k] is None else grads[k] - g
                pair_phi = pair_phi + row_phi.astype(F32)
            truth_phi = jnp.zeros((16, 128), F32)
            for m in range(members):
                p, g = parts(x[m] - truth)
                truth_phi = truth_phi + p.astype(F32)
                grad = weight * (g.astype(F32) - grads[m].astype(F32) * (1.0 / (members - 1)))
                grad_ref[m // per, m % per, rows, lanes] = grad.astype(BF16)
            share = weight * (truth_phi - pair_phi * (1.0 / (members - 1)) - self_phi)
            total = total + share[:8] + share[8:]
        return total

    share_ref[...] = lax.fori_loop(0, VPAD // 16, rows16, jnp.zeros((8, 128), F32))


def score(me, scale, every, truth, var_weight, area):
    devices, per = every.shape[:2]
    members = devices * per
    grid_spec = pltpu.PrefetchScalarGridSpec(
        num_scalar_prefetch=1,
        grid=(1,),
        in_specs=[
            pl.BlockSpec(memory_space=pltpu.SMEM),
            pl.BlockSpec(every.shape, lambda i, me: (0, 0, 0, 0)),
            pl.BlockSpec((VPAD, BLOCK), lambda i, me: (0, me[0])),
            pl.BlockSpec((VPAD, BLOCK), lambda i, me: (0, 0)),
            pl.BlockSpec((1, 1, BLOCK), lambda i, me: (me[0], 0, 0)),
        ],
        out_specs=[
            pl.BlockSpec(every.shape, lambda i, me: (0, 0, 0, 0)),
            pl.BlockSpec((8, 128), lambda i, me: (0, 0)),
        ],
    )

    def kernel(me_ref, *refs):
        score_kernel(members, *refs)

    return pl.pallas_call(
        kernel,
        grid_spec=grid_spec,
        out_shape=[
            jax.ShapeDtypeStruct(every.shape, BF16),
            jax.ShapeDtypeStruct((8, 128), F32),
        ],
        compiler_params=pltpu.CompilerParams(vmem_limit_bytes=SCORE_VMEM),
        name="score",
    )(me, scale, every, truth, var_weight, area)


def backward_kernel(
    core_ref, lat_ref, hidden_ref, slope_ref, up_ref, wout_ref, share_ref,
    gp_ref, mine_ref, other_ref, acc_in, acc_out, wide_ref,
):
    step, last = pl.program_id(0), pl.num_programs(0) - 1
    channels = lat_ref.shape[2]

    @pl.when(step == 0)
    def _():
        acc_in[...] = jnp.zeros_like(acc_in)
        acc_out[...] = jnp.zeros_like(acc_out)
        widen(wide_ref, wout_ref)

    for s in range(TILE // BLOCK):
        rows = pl.ds(s * BLOCK, BLOCK)
        block = jnp.concatenate(
            [up_ref[s, 0].astype(F32), jnp.zeros((WIDE - VPAD, BLOCK), F32)], axis=0
        )
        grad_hidden = jnp.dot(block.T.astype(BF16), wide_ref[...], preferred_element_type=F32)
        gp_ref[0, rows, :] = grad_hidden.astype(BF16) * slope_ref[0, rows, :]
    ups = jnp.concatenate([up_ref[s, 0] for s in range(TILE // BLOCK)], axis=1)
    acc_out[:VPAD, :] += jnp.dot(ups, hidden_ref[0], preferred_element_type=F32)
    product = lax.dot_general(
        lat_ref[0], gp_ref[0], (((0,), (0,)), ((), ())), preferred_element_type=F32
    )
    acc_in[...] += product.reshape(acc_in.shape)

    @pl.when(step == last)
    def _():
        core = core_ref[0]
        share = jnp.sum(share_ref[...])
        high = share.astype(BF16).astype(F32)
        middle = (share - high).astype(BF16).astype(F32)
        low = share - high - middle
        row = lax.broadcasted_iota(jnp.int32, acc_out.shape, 0) - (EXTRA + 3 * core)
        whole = jnp.where(
            row == 0,
            high,
            jnp.where(row == 1, middle, jnp.where(row == 2, low, acc_out[...])),
        )
        acc_out[...] = whole
        for chunk in range(channels // WIDE):
            piece = acc_out[:, chunk * WIDE : (chunk + 1) * WIDE].T.reshape(-1, 16, WIDE)
            for j in range(WIDE // 32):
                @pl.when(core == 0)
                def _():
                    mine_ref[chunk * 4 + j, :, channels:] = piece[2 * j].astype(BF16)
                    other_ref[chunk * 4 + j, :, channels:] = piece[2 * j + 1].astype(BF16)

                @pl.when(core == 1)
                def _():
                    mine_ref[chunk * 4 + j, :, channels:] = piece[2 * j + 1].astype(BF16)
                    other_ref[chunk * 4 + j, :, channels:] = piece[2 * j].astype(BF16)

        def group(g, carry):
            mine_ref[g, :, :channels] = acc_in[2 * g + core].astype(BF16)
            other_ref[g, :, :channels] = acc_in[2 * g + 1 - core].astype(BF16)
            return carry

        lax.fori_loop(0, channels // 32, group, 0, unroll=4)


def backward(core, latent, hidden, slopes, upstream, w_out_t, share):
    members, points, channels = latent.shape
    steps = points // TILE
    per = TILE // BLOCK
    tile = pl.BlockSpec((1, TILE, channels), lambda i, c: (i // steps, i % steps, 0))
    half = (channels // 32, 16, channels + WIDE)
    grid_spec = pltpu.PrefetchScalarGridSpec(
        num_scalar_prefetch=1,
        grid=(members * steps,),
        in_specs=[
            tile,
            tile,
            tile,
            pl.BlockSpec((per, 1, VPAD, BLOCK), lambda i, c: (i % steps, i // steps, 0, 0)),
            pl.BlockSpec(w_out_t.shape, lambda i, c: (0, 0)),
            pl.BlockSpec((8, 128), lambda i, c: (0, 0)),
        ],
        out_specs=[
            tile,
            pl.BlockSpec(half, lambda i, c: (0, 0, 0)),
            pl.BlockSpec(half, lambda i, c: (0, 0, 0)),
        ],
        scratch_shapes=[
            pltpu.VMEM((channels // 16, 16, channels), F32),
            pltpu.VMEM((WIDE, channels), F32),
            pltpu.VMEM((WIDE, channels), BF16),
        ],
    )
    return pl.pallas_call(
        backward_kernel,
        grid_spec=grid_spec,
        out_shape=[
            pltpu.HBM(latent.shape, BF16),
            jax.ShapeDtypeStruct(half, BF16),
            jax.ShapeDtypeStruct(half, BF16),
        ],
        compiler_params=pltpu.CompilerParams(vmem_limit_bytes=BACKWARD_VMEM),
        name="backward",
    )(core, in_hbm(latent), in_hbm(hidden), in_hbm(slopes), upstream, w_out_t, share)


def latent_kernel(gp_ref, win_ref, out_ref):
    for s in range(TILE // SUB):
        rows = pl.ds(s * SUB, SUB)
        out_ref[0, rows, :] = lax.dot_general(
            gp_ref[0, rows, :], win_ref[...], (((1,), (1,)), ((), ())), preferred_element_type=F32
        ).astype(BF16)


def latent_grad(gp, w_in):
    members, points, channels = gp.shape
    tile = pl.BlockSpec((1, TILE, channels), lambda m, i: (m, i, 0))
    return pl.pallas_call(
        latent_kernel,
        grid=(members, points // TILE),
        in_specs=[tile, pl.BlockSpec((channels, channels), lambda m, i: (0, 0))],
        out_specs=tile,
        out_shape=pltpu.HBM(gp.shape, BF16),
        compiler_params=pltpu.CompilerParams(vmem_limit_bytes=LATENT_VMEM),
        cost_estimate=pl.CostEstimate(
            flops=2 * members * points * channels * channels,
            bytes_accessed=4 * members * points * channels,
            transcendentals=0,
        ),
        name="latent_grad",
    )(in_hbm(gp), w_in)


def exchange(x, axis, xor):
    size = lax.axis_size(axis)
    return lax.ppermute(x, axis, [(i, i ^ xor) for i in range(size)])


def body(latent, w_in, w_out, targets, area_units, var_weight):
    date_count, per, points, channels = latent.shape
    variables = w_out.shape[1]
    member_devices = lax.axis_size("xh") * lax.axis_size("z")
    members = per * member_devices
    npoints = points * lax.axis_size("y") * lax.axis_size("core")
    dates = date_count * lax.axis_size("dp")
    me = (lax.axis_index("xh") * lax.axis_size("z") + lax.axis_index("z")).astype(jnp.int32)
    core = lax.axis_index("core").astype(jnp.int32)

    area_total = jnp.sum(area_units.astype(F32))
    for axis, xor in (("core", 1), ("y", 1), ("y", 2)):
        area_total = area_total + exchange(area_total, axis, xor)
    scale = (npoints / area_total).reshape(1, 1)

    rows = latent.reshape(date_count * per, points, channels)
    w_out_t = w_out.T
    preact, pred = forward(rows, w_in, w_out_t)
    every = lax.all_to_all(pred, MEMBER, 0, 0, tiled=True)
    hidden, slopes = shape(preact)
    truth = jnp.pad(targets[0], ((0, VPAD - variables), (0, 0)))
    var_wide = jnp.broadcast_to(
        jnp.pad(var_weight, (0, VPAD - variables))[:, None], (VPAD, BLOCK)
    )
    area = area_units.reshape(points // BLOCK, 1, BLOCK)
    grad_pred, share = score(me.reshape(1), scale, every, truth, var_wide, area)
    upstream = lax.all_to_all(grad_pred, MEMBER, 0, 0, tiled=True)
    gp, mine, other = backward(core.reshape(1), rows, hidden, slopes, upstream, w_out_t, share)
    wide = channels + WIDE
    both = (mine.astype(F32) + exchange(other, "core", 1).astype(F32)).astype(BF16)
    pieces = lax.all_to_all(both.reshape(-1, 8, wide), REST, 0, 0, tiled=True)
    grad_latent = latent_grad(gp, w_in)
    total = jnp.sum(pieces.astype(F32), axis=0)
    grad_scale = math.sqrt(dates * members * npoints)
    loss = jnp.sum(total[0, channels + EXTRA : channels + EXTRA + 6]) / (dates * npoints * variables)
    return (
        loss,
        grad_latent.reshape(latent.shape),
        total[:, :channels] / grad_scale,
        total[:, channels : channels + variables] / grad_scale,
    )


def solution(mesh):
    fine = Mesh(mesh.devices.reshape(2, 4, 4, 2, 2), ("xh", "z", "y", "core", "dp"))
    return jax.shard_map(
        body,
        mesh=fine,
        in_specs=(
            P("dp", MEMBER, ("y", "core"), None),
            P(),
            P(),
            P("dp", None, ("y", "core")),
            P(("y", "core")),
            P(),
        ),
        out_specs=(
            P(),
            P("dp", MEMBER, ("y", "core"), None),
            P(("xh", "z", "y", "core", "dp"), None),
            P(("xh", "z", "y", "core", "dp"), None),
        ),
        check_vma=False,
    )
```

```python
import functools
import math

import jax
import jax.numpy as jnp
from jax import lax
from jax.experimental import pallas as pl
from jax.experimental.pallas import tpu as pltpu
from jax.sharding import Mesh
from jax.sharding import PartitionSpec as P

GELU_C = 0.7978845608
GELU_A = 0.044715
SMOOTH = 0.01
BF16 = jnp.bfloat16
F32 = jnp.float32

BLOCK = 256
VPAD = 112
WIDE = 128
TILE = 1024
SUB = 256
EXTRA = 112

FORWARD_VMEM = 40 << 20
SHAPE_VMEM = 36 << 20
SCORE_VMEM = 16 << 20
BACKWARD_VMEM = 50 << 20
LATENT_VMEM = 40 << 20

MEMBER = ("xh", "z")
REST = ("xh", "z", "y", "dp")


def in_hbm(x):
    return pltpu.with_memory_space_constraint(x, pltpu.HBM)


def widen(wide_ref, wout_ref):
    variables = wout_ref.shape[0]
    wide_ref[...] = jnp.zeros_like(wide_ref)
    wide_ref[:variables, :] = wout_ref[...]


def forward_kernel(lat_ref, win_ref, wout_ref, preact_ref, pred_ref, wide_ref):
    @pl.when((pl.program_id(0) == 0) & (pl.program_id(1) == 0))
    def _():
        widen(wide_ref, wout_ref)

    for s in range(TILE // SUB):
        rows = pl.ds(s * SUB, SUB)
        u = jnp.dot(lat_ref[0, rows, :], win_ref[...], preferred_element_type=F32).astype(BF16)
        preact_ref[0, rows, :] = u
        bent = jnp.tanh(u * (BF16(GELU_C) + BF16(GELU_C * GELU_A) * (u * u)))
        twice = u + u * bent
        pred = lax.dot_general(
            twice, wide_ref[...], (((1,), (1,)), ((), ())), preferred_element_type=F32
        )
        pred_ref[s, 0] = (0.5 * pred.T[:VPAD]).astype(BF16)


def forward(latent, w_in, w_out_t):
    members, points, channels = latent.shape
    per = TILE // BLOCK
    tile = pl.BlockSpec((1, TILE, channels), lambda m, i: (m, i, 0))
    return pl.pallas_call(
        forward_kernel,
        grid=(members, points // TILE),
        in_specs=[
            tile,
            pl.BlockSpec((channels, channels), lambda m, i: (0, 0)),
            pl.BlockSpec(w_out_t.shape, lambda m, i: (0, 0)),
        ],
        out_specs=[
            tile,
            pl.BlockSpec((per, 1, VPAD, BLOCK), lambda m, i: (i, m, 0, 0)),
        ],
        out_shape=[
            pltpu.HBM(latent.shape, BF16),
            jax.ShapeDtypeStruct((points // BLOCK, members, VPAD, BLOCK), BF16),
        ],
        scratch_shapes=[pltpu.VMEM((WIDE, channels), BF16)],
        compiler_params=pltpu.CompilerParams(vmem_limit_bytes=FORWARD_VMEM),
        name="forward",
    )(in_hbm(latent), in_hbm(w_in), in_hbm(w_out_t))


def shape_kernel(preact_ref, hidden_ref, slope_ref):
    u = preact_ref[...].astype(F32)
    u2 = u * u
    half = 0.5 + 0.5 * jnp.tanh(u * (GELU_C + (GELU_C * GELU_A) * u2))
    value = u * half
    hidden_ref[...] = value.astype(BF16)
    bend = (2.0 * GELU_C) + (6.0 * GELU_A * GELU_C) * u2
    slope_ref[...] = (half + (value - value * half) * bend).astype(BF16)


def shape(preact):
    members, points, channels = preact.shape
    tile = pl.BlockSpec((1, TILE, channels), lambda m, i: (m, i, 0))
    return pl.pallas_call(
        shape_kernel,
        grid=(members, points // TILE),
        in_specs=[tile],
        out_specs=[tile, tile],
        out_shape=[pltpu.HBM(preact.shape, BF16)] * 2,
        compiler_params=pltpu.CompilerParams(vmem_limit_bytes=SHAPE_VMEM),
        cost_estimate=pl.CostEstimate(
            flops=16 * preact.size, bytes_accessed=6 * preact.size, transcendentals=preact.size
        ),
        name="shape",
    )(in_hbm(preact))


def score_kernel(
    members, scale_ref, pred_ref, truth_ref, var_ref, area_ref, grad_ref, share_ref, held_ref
):
    per = pred_ref.shape[1]
    scale = scale_ref[0, 0]
    self_phi = members * math.sqrt(SMOOTH) / (2.0 * (members - 1))

    @pl.when(pl.program_id(0) == 0)
    def _():
        share_ref[...] = jnp.zeros_like(share_ref)

    for lane in range(BLOCK // 128):
        lanes = pl.ds(lane * 128, 128)
        for half in range(2):
            rows = slice(8 * half, 8 * half + 8)
            truth = truth_ref[:, lanes].astype(F32)[rows]
            x = [pred_ref[m // per, m % per, :, lanes].astype(F32)[rows] - truth for m in range(members)]
            weight = (var_ref[:, lanes] * (area_ref[0, :, lanes].astype(F32) * scale))[rows]
            grads = [None] * members
            roots = None
            for m in range(members - 1):
                for k in range(m + 1, members):
                    d = x[m] - x[k]
                    r = lax.rsqrt(d * d + SMOOTH)
                    g = d * r
                    roots = r if roots is None else roots + r
                    grads[m] = g if grads[m] is None else grads[m] + g
                    grads[k] = -g if grads[k] is None else grads[k] - g
            score = None
            for m in range(members):
                q = x[m] * x[m] + SMOOTH
                r = lax.rsqrt(q)
                spread = grads[m] * (1.0 / (members - 1))
                mine = q * r - x[m] * spread
                score = mine if score is None else score + mine
                held_ref[m, rows, :] = weight * (x[m] * r - spread)
            score = score - roots * (SMOOTH / (members - 1)) - self_phi
            share_ref[...] += weight * score
        for m in range(members):
            grad_ref[m // per, m % per, :, lanes] = held_ref[m].astype(BF16)


def score(me, scale, every, truth, var_weight, area):
    devices, per = every.shape[:2]
    members = devices * per
    block = pl.BlockSpec((devices, per, 16, BLOCK), lambda i, me: (0, 0, i, 0))
    grid_spec = pltpu.PrefetchScalarGridSpec(
        num_scalar_prefetch=1,
        grid=(VPAD // 16,),
        in_specs=[
            pl.BlockSpec(memory_space=pltpu.SMEM),
            block,
            pl.BlockSpec((16, BLOCK), lambda i, me: (i, me[0])),
            pl.BlockSpec((16, BLOCK), lambda i, me: (i, 0)),
            pl.BlockSpec((1, 1, BLOCK), lambda i, me: (me[0], 0, 0)),
        ],
        out_specs=[block, pl.BlockSpec((8, 128), lambda i, me: (0, 0))],
        scratch_shapes=[pltpu.VMEM((members, 16, 128), F32)],
    )

    def kernel(me_ref, *refs):
        score_kernel(members, *refs)

    return pl.pallas_call(
        kernel,
        grid_spec=grid_spec,
        out_shape=[
            jax.ShapeDtypeStruct(every.shape, BF16),
            jax.ShapeDtypeStruct((8, 128), F32),
        ],
        compiler_params=pltpu.CompilerParams(vmem_limit_bytes=SCORE_VMEM),
        name="score",
    )(me, scale, every, truth, var_weight, area)


def preact_grad(up_ref, slope_ref, wide, s):
    block = jnp.concatenate(
        [up_ref[s, 0].astype(F32), jnp.zeros((WIDE - VPAD, BLOCK), F32)], axis=0
    )
    grad_hidden = jnp.dot(block.T.astype(BF16), wide, preferred_element_type=F32)
    return grad_hidden.astype(BF16) * slope_ref[0, pl.ds(s * BLOCK, BLOCK), :]


def backward_kernel(
    core_ref, lat_ref, hidden_ref, slope_ref, up_ref, wout_ref, share_ref,
    mine_ref, other_ref, acc_in, acc_out, wide_ref, gp_ref,
):
    step, last = pl.program_id(0), pl.num_programs(0) - 1
    channels = lat_ref.shape[2]

    @pl.when(step == 0)
    def _():
        acc_in[...] = jnp.zeros_like(acc_in)
        acc_out[...] = jnp.zeros_like(acc_out)
        widen(wide_ref, wout_ref)

    for s in range(TILE // BLOCK):
        gp_ref[pl.ds(s * BLOCK, BLOCK), :] = preact_grad(up_ref, slope_ref, wide_ref[...], s)
    ups = jnp.concatenate([up_ref[s, 0] for s in range(TILE // BLOCK)], axis=1)
    acc_out[:VPAD, :] += jnp.dot(ups, hidden_ref[0], preferred_element_type=F32)
    product = lax.dot_general(
        lat_ref[0], gp_ref[...], (((0,), (0,)), ((), ())), preferred_element_type=F32
    )
    acc_in[...] += product.reshape(acc_in.shape)

    @pl.when(step == last)
    def _():
        core = core_ref[0]
        share = jnp.sum(share_ref[...])
        high = share.astype(BF16).astype(F32)
        middle = (share - high).astype(BF16).astype(F32)
        low = share - high - middle
        row = lax.broadcasted_iota(jnp.int32, acc_out.shape, 0) - (EXTRA + 3 * core)
        acc_out[...] = jnp.where(
            row == 0,
            high,
            jnp.where(row == 1, middle, jnp.where(row == 2, low, acc_out[...])),
        )
        for chunk in range(channels // WIDE):
            piece = acc_out[:, chunk * WIDE : (chunk + 1) * WIDE].T.astype(BF16).reshape(-1, 16, WIDE)
            for j in range(WIDE // 32):
                @pl.when(core == 0)
                def _():
                    mine_ref[chunk * 4 + j, :, channels:] = piece[2 * j]
                    other_ref[chunk * 4 + j, :, channels:] = piece[2 * j + 1]

                @pl.when(core == 1)
                def _():
                    mine_ref[chunk * 4 + j, :, channels:] = piece[2 * j + 1]
                    other_ref[chunk * 4 + j, :, channels:] = piece[2 * j]

        def group(g, carry):
            mine_ref[g, :, :channels] = acc_in[2 * g + core].astype(BF16)
            other_ref[g, :, :channels] = acc_in[2 * g + 1 - core].astype(BF16)
            return carry

        lax.fori_loop(0, channels // 32, group, 0, unroll=4)


def backward(core, latent, hidden, slopes, upstream, w_out_t, share):
    members, points, channels = latent.shape
    steps = points // TILE
    per = TILE // BLOCK
    tile = pl.BlockSpec((1, TILE, channels), lambda i, c: (i // steps, i % steps, 0))
    half = (channels // 32, 16, channels + WIDE)
    grid_spec = pltpu.PrefetchScalarGridSpec(
        num_scalar_prefetch=1,
        grid=(members * steps,),
        in_specs=[
            tile,
            tile,
            tile,
            pl.BlockSpec((per, 1, VPAD, BLOCK), lambda i, c: (i % steps, i // steps, 0, 0)),
            pl.BlockSpec(w_out_t.shape, lambda i, c: (0, 0)),
            pl.BlockSpec((8, 128), lambda i, c: (0, 0)),
        ],
        out_specs=[pl.BlockSpec(half, lambda i, c: (0, 0, 0))] * 2,
        scratch_shapes=[
            pltpu.VMEM((channels // 16, 16, channels), F32),
            pltpu.VMEM((WIDE, channels), F32),
            pltpu.VMEM((WIDE, channels), BF16),
            pltpu.VMEM((TILE, channels), BF16),
        ],
    )
    return pl.pallas_call(
        backward_kernel,
        grid_spec=grid_spec,
        out_shape=[jax.ShapeDtypeStruct(half, BF16)] * 2,
        compiler_params=pltpu.CompilerParams(vmem_limit_bytes=BACKWARD_VMEM),
        name="backward",
    )(core, in_hbm(latent), in_hbm(hidden), in_hbm(slopes), upstream, in_hbm(w_out_t), share)


def latent_kernel(slope_ref, up_ref, wout_ref, win_ref, out_ref, wide_ref):
    @pl.when((pl.program_id(0) == 0) & (pl.program_id(1) == 0))
    def _():
        widen(wide_ref, wout_ref)

    for s in range(TILE // BLOCK):
        out_ref[0, pl.ds(s * BLOCK, BLOCK), :] = lax.dot_general(
            preact_grad(up_ref, slope_ref, wide_ref[...], s),
            win_ref[...],
            (((1,), (1,)), ((), ())),
            preferred_element_type=F32,
        ).astype(BF16)


def latent_grad(slopes, upstream, w_out_t, w_in):
    members, points, channels = slopes.shape
    per = TILE // BLOCK
    tile = pl.BlockSpec((1, TILE, channels), lambda m, i: (m, i, 0))
    return pl.pallas_call(
        latent_kernel,
        grid=(members, points // TILE),
        in_specs=[
            tile,
            pl.BlockSpec((per, 1, VPAD, BLOCK), lambda m, i: (i, m, 0, 0)),
            pl.BlockSpec(w_out_t.shape, lambda m, i: (0, 0)),
            pl.BlockSpec((channels, channels), lambda m, i: (0, 0)),
        ],
        out_specs=tile,
        out_shape=pltpu.HBM(slopes.shape, BF16),
        scratch_shapes=[pltpu.VMEM((WIDE, channels), BF16)],
        compiler_params=pltpu.CompilerParams(vmem_limit_bytes=LATENT_VMEM),
        cost_estimate=pl.CostEstimate(
            flops=2 * members * points * channels * (channels + WIDE),
            bytes_accessed=4 * members * points * channels,
            transcendentals=0,
        ),
        name="latent_grad",
    )(in_hbm(slopes), upstream, in_hbm(w_out_t), in_hbm(w_in))


def finish_kernel(grad_scale, loss_scale, pieces_ref, in_ref, out_ref, loss_ref):
    channels, variables = in_ref.shape[1], out_ref.shape[1]
    total = pieces_ref[0].astype(F32)
    for p in range(1, pieces_ref.shape[0]):
        total = total + pieces_ref[p].astype(F32)
    in_ref[...] = total[:, :channels] / grad_scale
    out_ref[...] = total[:, channels : channels + variables] / grad_scale
    tail = total[:1, channels:]
    column = lax.broadcasted_iota(jnp.int32, tail.shape, 1)
    loss_ref[0, 0] = jnp.sum(jnp.where(column >= EXTRA, tail, 0.0)) / loss_scale


def finish(pieces, variables, grad_scale, loss_scale):
    rows, wide = pieces.shape[1:]
    channels = wide - WIDE
    return pl.pallas_call(
        functools.partial(finish_kernel, grad_scale, loss_scale),
        out_specs=[
            pl.BlockSpec(memory_space=pltpu.VMEM),
            pl.BlockSpec(memory_space=pltpu.VMEM),
            pl.BlockSpec(memory_space=pltpu.SMEM),
        ],
        out_shape=[
            jax.ShapeDtypeStruct((rows, channels), F32),
            jax.ShapeDtypeStruct((rows, variables), F32),
            jax.ShapeDtypeStruct((1, 1), F32),
        ],
        compiler_params=pltpu.CompilerParams(vmem_limit_bytes=16 << 20),
        name="finish",
    )(pieces)


def exchange(x, axis, xor):
    size = lax.axis_size(axis)
    return lax.ppermute(x, axis, [(i, i ^ xor) for i in range(size)])


def body(latent, w_in, w_out, targets, area_units, var_weight):
    date_count, per, points, channels = latent.shape
    variables = w_out.shape[1]
    member_devices = lax.axis_size("xh") * lax.axis_size("z")
    members = per * member_devices
    npoints = points * lax.axis_size("y") * lax.axis_size("core")
    dates = date_count * lax.axis_size("dp")
    me = (lax.axis_index("xh") * lax.axis_size("z") + lax.axis_index("z")).astype(jnp.int32)
    core = lax.axis_index("core").astype(jnp.int32)

    area_total = jnp.sum(area_units.astype(F32))
    for axis, xor in (("core", 1), ("y", 1), ("y", 2)):
        area_total = area_total + exchange(area_total, axis, xor)
    scale = (npoints / area_total).reshape(1, 1)

    rows = latent.reshape(date_count * per, points, channels)
    w_out_t = w_out.T
    preact, pred = forward(rows, w_in, w_out_t)
    every = lax.all_to_all(pred, MEMBER, 0, 0, tiled=True)
    hidden, slopes = shape(preact)
    truth = jnp.pad(targets[0], ((0, VPAD - variables), (0, 0)))
    var_wide = jnp.broadcast_to(
        jnp.pad(var_weight, (0, VPAD - variables))[:, None], (VPAD, BLOCK)
    )
    area = area_units.reshape(points // BLOCK, 1, BLOCK)
    grad_pred, share = score(me.reshape(1), scale, every, truth, var_wide, area)
    upstream = lax.all_to_all(grad_pred, MEMBER, 0, 0, tiled=True)
    mine, other = backward(core.reshape(1), rows, hidden, slopes, upstream, w_out_t, share)
    wide = channels + WIDE
    both = (mine.astype(F32) + exchange(other, "core", 1).astype(F32)).astype(BF16)
    pieces = lax.all_to_all(both.reshape(-1, 8, wide), REST, 0, 0, tiled=True)
    grad_latent = latent_grad(slopes, upstream, w_out_t, w_in)
    grad_scale = math.sqrt(dates * members * npoints)
    grad_in, grad_out, loss = finish(pieces, variables, grad_scale, dates * npoints * variables)
    return loss.reshape(()), grad_latent.reshape(latent.shape), grad_in, grad_out


def solution(mesh):
    fine = Mesh(mesh.devices.reshape(2, 4, 4, 2, 2), ("xh", "z", "y", "core", "dp"))
    return jax.shard_map(
        body,
        mesh=fine,
        in_specs=(
            P("dp", MEMBER, ("y", "core"), None),
            P(),
            P(),
            P("dp", None, ("y", "core")),
            P(("y", "core")),
            P(),
        ),
        out_specs=(
            P(),
            P("dp", MEMBER, ("y", "core"), None),
            P(("xh", "z", "y", "core", "dp"), None),
            P(("xh", "z", "y", "core", "dp"), None),
        ),
        check_vma=False,
    )
```

```python
import functools
import math

import jax
import jax.numpy as jnp
from jax import lax
from jax.experimental import pallas as pl
from jax.experimental.pallas import tpu as pltpu
from jax.sharding import Mesh
from jax.sharding import PartitionSpec as P

GELU_C = 0.7978845608
GELU_A = 0.044715
SMOOTH = 0.01
BF16 = jnp.bfloat16
F32 = jnp.float32

BLOCK = 256
VPAD = 104
WIDE = 128
TILE = 1024
SUB = 256
EXTRA = 112

FORWARD_VMEM = 40 << 20
SHAPE_VMEM = 36 << 20
SCORE_VMEM = 16 << 20
BACKWARD_VMEM = 50 << 20
LATENT_VMEM = 40 << 20

MEMBER = ("xh", "z")
REST = ("xh", "z", "y", "dp")


def in_hbm(x):
    return pltpu.with_memory_space_constraint(x, pltpu.HBM)


def widen(wide_ref, wout_ref):
    variables = wout_ref.shape[0]
    wide_ref[...] = jnp.zeros_like(wide_ref)
    wide_ref[:variables, :] = wout_ref[...]


def forward_kernel(lat_ref, win_ref, wout_ref, preact_ref, pred_ref, wide_ref):
    @pl.when((pl.program_id(0) == 0) & (pl.program_id(1) == 0))
    def _():
        widen(wide_ref, wout_ref)

    for s in range(TILE // SUB):
        rows = pl.ds(s * SUB, SUB)
        u = jnp.dot(lat_ref[0, rows, :], win_ref[...], preferred_element_type=F32).astype(BF16)
        preact_ref[0, rows, :] = u
        bent = jnp.tanh(u * (BF16(GELU_C) + BF16(GELU_C * GELU_A) * (u * u)))
        twice = u + u * bent
        pred = lax.dot_general(
            twice, wide_ref[...], (((1,), (1,)), ((), ())), preferred_element_type=F32
        )
        pred_ref[s, 0] = (0.5 * pred.T[:VPAD]).astype(BF16)


def forward(latent, w_in, w_out_t):
    members, points, channels = latent.shape
    per = TILE // BLOCK
    tile = pl.BlockSpec((1, TILE, channels), lambda m, i: (m, i, 0))
    return pl.pallas_call(
        forward_kernel,
        grid=(members, points // TILE),
        in_specs=[
            tile,
            pl.BlockSpec((channels, channels), lambda m, i: (0, 0)),
            pl.BlockSpec(w_out_t.shape, lambda m, i: (0, 0)),
        ],
        out_specs=[
            tile,
            pl.BlockSpec((per, 1, VPAD, BLOCK), lambda m, i: (i, m, 0, 0)),
        ],
        out_shape=[
            pltpu.HBM(latent.shape, BF16),
            jax.ShapeDtypeStruct((points // BLOCK, members, VPAD, BLOCK), BF16),
        ],
        scratch_shapes=[pltpu.VMEM((WIDE, channels), BF16)],
        compiler_params=pltpu.CompilerParams(vmem_limit_bytes=FORWARD_VMEM),
        name="forward",
    )(in_hbm(latent), in_hbm(w_in), in_hbm(w_out_t))


def shape_kernel(preact_ref, hidden_ref, slope_ref):
    u = preact_ref[...].astype(F32)
    u2 = u * u
    half = 0.5 + 0.5 * jnp.tanh(u * (GELU_C + (GELU_C * GELU_A) * u2))
    value = u * half
    hidden_ref[...] = value.astype(BF16)
    bend = (2.0 * GELU_C) + (6.0 * GELU_A * GELU_C) * u2
    slope_ref[...] = (half + (value - value * half) * bend).astype(BF16)


def shape(preact):
    members, points, channels = preact.shape
    tile = pl.BlockSpec((1, TILE, channels), lambda m, i: (m, i, 0))
    return pl.pallas_call(
        shape_kernel,
        grid=(members, points // TILE),
        in_specs=[tile],
        out_specs=[tile, tile],
        out_shape=[pltpu.HBM(preact.shape, BF16)] * 2,
        compiler_params=pltpu.CompilerParams(vmem_limit_bytes=SHAPE_VMEM),
        cost_estimate=pl.CostEstimate(
            flops=16 * preact.size, bytes_accessed=6 * preact.size, transcendentals=preact.size
        ),
        name="shape",
    )(in_hbm(preact))


def score_kernel(
    members, scale_ref, pred_ref, truth_ref, var_ref, area_ref, grad_ref, share_ref, held_ref, true_ref
):
    per = pred_ref.shape[1]
    scale = scale_ref[0, 0]
    self_phi = members * math.sqrt(SMOOTH) / (2.0 * (members - 1))
    true_ref[...] = truth_ref[...].astype(F32)
    for m in range(members):
        held_ref[m] = pred_ref[m // per, m % per].astype(F32)

    def part(rows, lanes):
        truth = true_ref[rows, lanes]
        x = [held_ref[m, rows, lanes] - truth for m in range(members)]
        weight = var_ref[rows, lanes] * (area_ref[0, :, lanes].astype(F32) * scale)
        grads = [None] * members
        roots = None
        for m in range(members - 1):
            for k in range(m + 1, members):
                d = x[m] - x[k]
                r = lax.rsqrt(d * d + SMOOTH)
                g = d * r
                roots = r if roots is None else roots + r
                grads[m] = g if grads[m] is None else grads[m] + g
                grads[k] = -g if grads[k] is None else grads[k] - g
        score = None
        for m in range(members):
            q = x[m] * x[m] + SMOOTH
            r = lax.rsqrt(q)
            spread = grads[m] * (1.0 / (members - 1))
            mine = q * r - x[m] * spread
            score = mine if score is None else score + mine
            held_ref[m, rows, lanes] = weight * (x[m] * r - spread)
        return weight * (score - roots * (SMOOTH / (members - 1)) - self_phi)

    def rows8(step, total):
        rows = pl.ds(pl.multiple_of(step * 8, 8), 8)
        for lane in range(BLOCK // 128):
            total = total + part(rows, pl.ds(lane * 128, 128))
        return total

    share_ref[...] = lax.fori_loop(0, VPAD // 8, rows8, jnp.zeros((8, 128), F32))
    for m in range(members):
        grad_ref[m // per, m % per] = held_ref[m].astype(BF16)


def score(me, scale, every, truth, var_weight, area):
    devices, per = every.shape[:2]
    members = devices * per
    vmem = pl.BlockSpec(memory_space=pltpu.VMEM)
    grid_spec = pltpu.PrefetchScalarGridSpec(
        num_scalar_prefetch=1,
        grid=(1,),
        in_specs=[
            pl.BlockSpec(memory_space=pltpu.SMEM),
            vmem,
            pl.BlockSpec((VPAD, BLOCK), lambda i, me: (0, me[0])),
            vmem,
            pl.BlockSpec((1, 1, BLOCK), lambda i, me: (me[0], 0, 0)),
        ],
        out_specs=[vmem, vmem],
        scratch_shapes=[
            pltpu.VMEM((members, VPAD, BLOCK), F32),
            pltpu.VMEM((VPAD, BLOCK), F32),
        ],
    )

    def kernel(me_ref, *refs):
        score_kernel(members, *refs)

    return pl.pallas_call(
        kernel,
        grid_spec=grid_spec,
        out_shape=[
            jax.ShapeDtypeStruct(every.shape, BF16),
            jax.ShapeDtypeStruct((8, 128), F32),
        ],
        compiler_params=pltpu.CompilerParams(vmem_limit_bytes=SCORE_VMEM),
        name="score",
    )(me, scale, every, truth, var_weight, area)


def preact_grad(up_ref, slope_ref, wide, s):
    block = jnp.concatenate(
        [up_ref[s, 0].astype(F32), jnp.zeros((WIDE - VPAD, BLOCK), F32)], axis=0
    )
    grad_hidden = jnp.dot(block.T.astype(BF16), wide, preferred_element_type=F32)
    return grad_hidden.astype(BF16) * slope_ref[0, pl.ds(s * BLOCK, BLOCK), :]


def backward_kernel(
    core_ref, lat_ref, hidden_ref, slope_ref, up_ref, wout_ref, share_ref,
    mine_ref, other_ref, acc_in, acc_out, wide_ref, gp_ref,
):
    step, last = pl.program_id(0), pl.num_programs(0) - 1
    channels = lat_ref.shape[2]

    @pl.when(step == 0)
    def _():
        acc_in[...] = jnp.zeros_like(acc_in)
        acc_out[...] = jnp.zeros_like(acc_out)
        widen(wide_ref, wout_ref)

    for s in range(TILE // BLOCK):
        gp_ref[pl.ds(s * BLOCK, BLOCK), :] = preact_grad(up_ref, slope_ref, wide_ref[...], s)
    ups = jnp.concatenate([up_ref[s, 0] for s in range(TILE // BLOCK)], axis=1)
    acc_out[:VPAD, :] += jnp.dot(ups, hidden_ref[0], preferred_element_type=F32)
    product = lax.dot_general(
        lat_ref[0], gp_ref[...], (((0,), (0,)), ((), ())), preferred_element_type=F32
    )
    acc_in[...] += product.reshape(acc_in.shape)

    @pl.when(step == last)
    def _():
        core = core_ref[0]
        share = jnp.sum(share_ref[...])
        high = share.astype(BF16).astype(F32)
        middle = (share - high).astype(BF16).astype(F32)
        low = share - high - middle
        row = lax.broadcasted_iota(jnp.int32, acc_out.shape, 0) - (EXTRA + 3 * core)
        acc_out[...] = jnp.where(
            row == 0,
            high,
            jnp.where(row == 1, middle, jnp.where(row == 2, low, acc_out[...])),
        )
        for chunk in range(channels // WIDE):
            piece = acc_out[:, chunk * WIDE : (chunk + 1) * WIDE].T.astype(BF16).reshape(-1, 16, WIDE)
            for j in range(WIDE // 32):
                @pl.when(core == 0)
                def _():
                    mine_ref[chunk * 4 + j, :, channels:] = piece[2 * j]
                    other_ref[chunk * 4 + j, :, channels:] = piece[2 * j + 1]

                @pl.when(core == 1)
                def _():
                    mine_ref[chunk * 4 + j, :, channels:] = piece[2 * j + 1]
                    other_ref[chunk * 4 + j, :, channels:] = piece[2 * j]

        def group(g, carry):
            mine_ref[g, :, :channels] = acc_in[2 * g + core].astype(BF16)
            other_ref[g, :, :channels] = acc_in[2 * g + 1 - core].astype(BF16)
            return carry

        lax.fori_loop(0, channels // 32, group, 0, unroll=4)


def backward(core, latent, hidden, slopes, upstream, w_out_t, share):
    members, points, channels = latent.shape
    steps = points // TILE
    per = TILE // BLOCK
    tile = pl.BlockSpec((1, TILE, channels), lambda i, c: (i // steps, i % steps, 0))
    half = (channels // 32, 16, channels + WIDE)
    grid_spec = pltpu.PrefetchScalarGridSpec(
        num_scalar_prefetch=1,
        grid=(members * steps,),
        in_specs=[
            tile,
            tile,
            tile,
            pl.BlockSpec((per, 1, VPAD, BLOCK), lambda i, c: (i % steps, i // steps, 0, 0)),
            pl.BlockSpec(w_out_t.shape, lambda i, c: (0, 0)),
            pl.BlockSpec((8, 128), lambda i, c: (0, 0)),
        ],
        out_specs=[pl.BlockSpec(half, lambda i, c: (0, 0, 0))] * 2,
        scratch_shapes=[
            pltpu.VMEM((channels // 16, 16, channels), F32),
            pltpu.VMEM((WIDE, channels), F32),
            pltpu.VMEM((WIDE, channels), BF16),
            pltpu.VMEM((TILE, channels), BF16),
        ],
    )
    return pl.pallas_call(
        backward_kernel,
        grid_spec=grid_spec,
        out_shape=[jax.ShapeDtypeStruct(half, BF16)] * 2,
        compiler_params=pltpu.CompilerParams(vmem_limit_bytes=BACKWARD_VMEM),
        name="backward",
    )(core, in_hbm(latent), in_hbm(hidden), in_hbm(slopes), upstream, in_hbm(w_out_t), share)


def latent_kernel(slope_ref, up_ref, wout_ref, win_ref, out_ref, wide_ref):
    @pl.when((pl.program_id(0) == 0) & (pl.program_id(1) == 0))
    def _():
        widen(wide_ref, wout_ref)

    for s in range(TILE // BLOCK):
        out_ref[0, pl.ds(s * BLOCK, BLOCK), :] = lax.dot_general(
            preact_grad(up_ref, slope_ref, wide_ref[...], s),
            win_ref[...],
            (((1,), (1,)), ((), ())),
            preferred_element_type=F32,
        ).astype(BF16)


def latent_grad(slopes, upstream, w_out_t, w_in):
    members, points, channels = slopes.shape
    per = TILE // BLOCK
    tile = pl.BlockSpec((1, TILE, channels), lambda m, i: (m, i, 0))
    return pl.pallas_call(
        latent_kernel,
        grid=(members, points // TILE),
        in_specs=[
            tile,
            pl.BlockSpec((per, 1, VPAD, BLOCK), lambda m, i: (i, m, 0, 0)),
            pl.BlockSpec(w_out_t.shape, lambda m, i: (0, 0)),
            pl.BlockSpec((channels, channels), lambda m, i: (0, 0)),
        ],
        out_specs=tile,
        out_shape=pltpu.HBM(slopes.shape, BF16),
        scratch_shapes=[pltpu.VMEM((WIDE, channels), BF16)],
        compiler_params=pltpu.CompilerParams(vmem_limit_bytes=LATENT_VMEM),
        cost_estimate=pl.CostEstimate(
            flops=2 * members * points * channels * (channels + WIDE),
            bytes_accessed=4 * members * points * channels,
            transcendentals=0,
        ),
        name="latent_grad",
    )(in_hbm(slopes), upstream, in_hbm(w_out_t), in_hbm(w_in))


def finish_kernel(grad_scale, loss_scale, pieces_ref, in_ref, out_ref, loss_ref):
    channels, variables = in_ref.shape[1], out_ref.shape[1]
    total = pieces_ref[0].astype(F32)
    for p in range(1, pieces_ref.shape[0]):
        total = total + pieces_ref[p].astype(F32)
    in_ref[...] = total[:, :channels] / grad_scale
    out_ref[...] = total[:, channels : channels + variables] / grad_scale
    tail = total[:1, channels:]
    column = lax.broadcasted_iota(jnp.int32, tail.shape, 1)
    loss_ref[0, 0] = jnp.sum(jnp.where(column >= EXTRA, tail, 0.0)) / loss_scale


def finish(pieces, variables, grad_scale, loss_scale):
    rows, wide = pieces.shape[1:]
    channels = wide - WIDE
    return pl.pallas_call(
        functools.partial(finish_kernel, grad_scale, loss_scale),
        out_specs=[
            pl.BlockSpec(memory_space=pltpu.VMEM),
            pl.BlockSpec(memory_space=pltpu.VMEM),
            pl.BlockSpec(memory_space=pltpu.SMEM),
        ],
        out_shape=[
            jax.ShapeDtypeStruct((rows, channels), F32),
            jax.ShapeDtypeStruct((rows, variables), F32),
            jax.ShapeDtypeStruct((1, 1), F32),
        ],
        compiler_params=pltpu.CompilerParams(vmem_limit_bytes=16 << 20),
        name="finish",
    )(pieces)


def exchange(x, axis, xor):
    size = lax.axis_size(axis)
    return lax.ppermute(x, axis, [(i, i ^ xor) for i in range(size)])


def body(latent, w_in, w_out, targets, area_units, var_weight):
    date_count, per, points, channels = latent.shape
    variables = w_out.shape[1]
    member_devices = lax.axis_size("xh") * lax.axis_size("z")
    members = per * member_devices
    npoints = points * lax.axis_size("y") * lax.axis_size("core")
    dates = date_count * lax.axis_size("dp")
    me = (lax.axis_index("xh") * lax.axis_size("z") + lax.axis_index("z")).astype(jnp.int32)
    core = lax.axis_index("core").astype(jnp.int32)

    area_total = jnp.sum(area_units.astype(F32))
    for axis, xor in (("core", 1), ("y", 1), ("y", 3)):
        area_total = area_total + exchange(area_total, axis, xor)
    scale = (npoints / area_total).reshape(1, 1)

    rows = latent.reshape(date_count * per, points, channels)
    w_out_t = w_out.T
    preact, pred = forward(rows, w_in, w_out_t)
    every = lax.all_to_all(pred, MEMBER, 0, 0, tiled=True)
    hidden, slopes = shape(preact)
    truth = jnp.pad(targets[0], ((0, VPAD - variables), (0, 0)))
    var_wide = jnp.broadcast_to(
        jnp.pad(var_weight, (0, VPAD - variables))[:, None], (VPAD, BLOCK)
    )
    area = area_units.reshape(points // BLOCK, 1, BLOCK)
    grad_pred, share = score(me.reshape(1), scale, every, truth, var_wide, area)
    upstream = lax.all_to_all(grad_pred, MEMBER, 0, 0, tiled=True)
    mine, other = backward(core.reshape(1), rows, hidden, slopes, upstream, w_out_t, share)
    wide = channels + WIDE
    both = (mine.astype(F32) + exchange(other, "core", 1).astype(F32)).astype(BF16)
    pieces = lax.all_to_all(both.reshape(-1, 8, wide), REST, 0, 0, tiled=True)
    grad_latent = latent_grad(slopes, upstream, w_out_t, w_in)
    grad_scale = math.sqrt(dates * members * npoints)
    grad_in, grad_out, loss = finish(pieces, variables, grad_scale, dates * npoints * variables)
    return loss.reshape(()), grad_latent.reshape(latent.shape), grad_in, grad_out


def solution(mesh):
    fine = Mesh(mesh.devices.reshape(2, 4, 4, 2, 2), ("xh", "z", "y", "core", "dp"))
    return jax.shard_map(
        body,
        mesh=fine,
        in_specs=(
            P("dp", MEMBER, ("y", "core"), None),
            P(),
            P(),
            P("dp", None, ("y", "core")),
            P(("y", "core")),
            P(),
        ),
        out_specs=(
            P(),
            P("dp", MEMBER, ("y", "core"), None),
            P(("xh", "z", "y", "core", "dp"), None),
            P(("xh", "z", "y", "core", "dp"), None),
        ),
        check_vma=False,
    )
```

```python
import functools
import math

import jax
import jax.numpy as jnp
from jax import lax
from jax.experimental import pallas as pl
from jax.experimental.pallas import tpu as pltpu
from jax.sharding import Mesh
from jax.sharding import PartitionSpec as P

GELU_C = 0.7978845608
GELU_A = 0.044715
SMOOTH = 0.01
BF16 = jnp.bfloat16
F32 = jnp.float32

SHAPE_TILE = 2048
BLOCK = 256
VPAD = 104
WIDE = 128
TILE = 1024
SUB = 256
EXTRA = 112

FORWARD_VMEM = 40 << 20
SHAPE_VMEM = 44 << 20
SCORE_VMEM = 16 << 20
BACKWARD_VMEM = 50 << 20
LATENT_VMEM = 40 << 20

MEMBER = ("xh", "z")
REST = ("xh", "z", "y", "dp")


def in_hbm(x):
    return pltpu.with_memory_space_constraint(x, pltpu.HBM)


def widen(wide_ref, wout_ref):
    variables = wout_ref.shape[0]
    wide_ref[...] = jnp.zeros_like(wide_ref)
    wide_ref[:variables, :] = wout_ref[...]


def forward_kernel(lat_ref, win_ref, wout_ref, preact_ref, pred_ref, wide_ref):
    @pl.when((pl.program_id(0) == 0) & (pl.program_id(1) == 0))
    def _():
        widen(wide_ref, wout_ref)

    for s in range(TILE // SUB):
        rows = pl.ds(s * SUB, SUB)
        u = jnp.dot(lat_ref[0, rows, :], win_ref[...], preferred_element_type=F32).astype(BF16)
        preact_ref[0, rows, :] = u
        bent = jnp.tanh(u * (BF16(GELU_C) + BF16(GELU_C * GELU_A) * (u * u)))
        twice = u + u * bent
        pred = lax.dot_general(
            twice, wide_ref[...], (((1,), (1,)), ((), ())), preferred_element_type=F32
        )
        pred_ref[s, 0] = (0.5 * pred.T[:VPAD]).astype(BF16)


def forward(latent, w_in, w_out_t):
    members, points, channels = latent.shape
    per = TILE // BLOCK
    tile = pl.BlockSpec((1, TILE, channels), lambda m, i: (m, i, 0))
    return pl.pallas_call(
        forward_kernel,
        grid=(members, points // TILE),
        in_specs=[
            tile,
            pl.BlockSpec((channels, channels), lambda m, i: (0, 0)),
            pl.BlockSpec(w_out_t.shape, lambda m, i: (0, 0)),
        ],
        out_specs=[
            tile,
            pl.BlockSpec((per, 1, VPAD, BLOCK), lambda m, i: (i, m, 0, 0)),
        ],
        out_shape=[
            pltpu.HBM(latent.shape, BF16),
            jax.ShapeDtypeStruct((points // BLOCK, members, VPAD, BLOCK), BF16),
        ],
        scratch_shapes=[pltpu.VMEM((WIDE, channels), BF16)],
        compiler_params=pltpu.CompilerParams(vmem_limit_bytes=FORWARD_VMEM),
        name="forward",
    )(in_hbm(latent), in_hbm(w_in), in_hbm(w_out_t))


def shape_kernel(preact_ref, hidden_ref, slope_ref):
    for s in range(SHAPE_TILE // SUB):
        rows = pl.ds(s * SUB, SUB)
        u = preact_ref[0, rows, :]
        u2 = u * u
        bent = jnp.tanh(u * (BF16(GELU_C) + BF16(GELU_C * GELU_A) * u2))
        half = BF16(0.5) + BF16(0.5) * bent
        value = u * half
        hidden_ref[0, rows, :] = value
        bend = BF16(GELU_C) + BF16(3.0 * GELU_A * GELU_C) * u2
        slope_ref[0, rows, :] = half + value * ((BF16(1.0) - bent) * bend)


def shape(preact):
    members, points, channels = preact.shape
    tile = pl.BlockSpec((1, SHAPE_TILE, channels), lambda m, i: (m, i, 0))
    return pl.pallas_call(
        shape_kernel,
        grid=(members, points // SHAPE_TILE),
        in_specs=[tile],
        out_specs=[tile, tile],
        out_shape=[pltpu.HBM(preact.shape, BF16)] * 2,
        compiler_params=pltpu.CompilerParams(vmem_limit_bytes=SHAPE_VMEM),
        cost_estimate=pl.CostEstimate(
            flops=16 * preact.size, bytes_accessed=6 * preact.size, transcendentals=preact.size
        ),
        name="shape",
    )(in_hbm(preact))


def score_kernel(
    members, scale_ref, pred_ref, truth_ref, var_ref, area_ref, grad_ref, share_ref, held_ref, true_ref
):
    per = pred_ref.shape[1]
    scale = scale_ref[0, 0]
    self_phi = members * math.sqrt(SMOOTH) / (2.0 * (members - 1))
    true_ref[...] = truth_ref[...].astype(F32)
    for m in range(members):
        held_ref[m] = pred_ref[m // per, m % per].astype(F32)

    def part(rows, lanes):
        truth = true_ref[rows, lanes]
        x = [held_ref[m, rows, lanes] - truth for m in range(members)]
        weight = var_ref[rows, lanes] * (area_ref[0, :, lanes].astype(F32) * scale)
        grads = [None] * members
        roots = None
        for m in range(members - 1):
            for k in range(m + 1, members):
                d = x[m] - x[k]
                r = lax.rsqrt(d * d + SMOOTH)
                g = d * r
                roots = r if roots is None else roots + r
                grads[m] = g if grads[m] is None else grads[m] + g
                grads[k] = -g if grads[k] is None else grads[k] - g
        score = None
        for m in range(members):
            q = x[m] * x[m] + SMOOTH
            r = lax.rsqrt(q)
            spread = grads[m] * (1.0 / (members - 1))
            mine = q * r - x[m] * spread
            score = mine if score is None else score + mine
            held_ref[m, rows, lanes] = weight * (x[m] * r - spread)
        return weight * (score - roots * (SMOOTH / (members - 1)) - self_phi)

    def rows8(step, total):
        rows = pl.ds(pl.multiple_of(step * 8, 8), 8)
        for lane in range(BLOCK // 128):
            total = total + part(rows, pl.ds(lane * 128, 128))
        return total

    share_ref[...] = lax.fori_loop(0, VPAD // 8, rows8, jnp.zeros((8, 128), F32))
    for m in range(members):
        grad_ref[m // per, m % per] = held_ref[m].astype(BF16)


def score(me, scale, every, truth, var_weight, area):
    devices, per = every.shape[:2]
    members = devices * per
    vmem = pl.BlockSpec(memory_space=pltpu.VMEM)
    grid_spec = pltpu.PrefetchScalarGridSpec(
        num_scalar_prefetch=1,
        grid=(1,),
        in_specs=[
            pl.BlockSpec(memory_space=pltpu.SMEM),
            vmem,
            pl.BlockSpec((VPAD, BLOCK), lambda i, me: (0, me[0])),
            vmem,
            pl.BlockSpec((1, 1, BLOCK), lambda i, me: (me[0], 0, 0)),
        ],
        out_specs=[vmem, vmem],
        scratch_shapes=[
            pltpu.VMEM((members, VPAD, BLOCK), F32),
            pltpu.VMEM((VPAD, BLOCK), F32),
        ],
    )

    def kernel(me_ref, *refs):
        score_kernel(members, *refs)

    return pl.pallas_call(
        kernel,
        grid_spec=grid_spec,
        out_shape=[
            jax.ShapeDtypeStruct(every.shape, BF16),
            jax.ShapeDtypeStruct((8, 128), F32),
        ],
        compiler_params=pltpu.CompilerParams(vmem_limit_bytes=SCORE_VMEM),
        name="score",
    )(me, scale, every, truth, var_weight, area)


def preact_grad(up_ref, slope_ref, wide, s):
    block = jnp.concatenate(
        [up_ref[s, 0].astype(F32), jnp.zeros((WIDE - VPAD, BLOCK), F32)], axis=0
    )
    grad_hidden = jnp.dot(block.T.astype(BF16), wide, preferred_element_type=F32)
    return grad_hidden.astype(BF16) * slope_ref[0, pl.ds(s * BLOCK, BLOCK), :]


def backward_kernel(
    core_ref, lat_ref, hidden_ref, slope_ref, up_ref, wout_ref, share_ref,
    mine_ref, other_ref, acc_in, acc_out, tail_ref, wide_ref, gp_ref,
):
    step, last = pl.program_id(0), pl.num_programs(0) - 1
    channels = lat_ref.shape[2]

    @pl.when(step == 0)
    def _():
        widen(wide_ref, wout_ref)

    def onward(acc):
        return jnp.where(step == 0, 0.0, acc[...])

    for s in range(TILE // BLOCK):
        gp_ref[pl.ds(s * BLOCK, BLOCK), :] = preact_grad(up_ref, slope_ref, wide_ref[...], s)
    ups = jnp.concatenate([up_ref[s, 0] for s in range(TILE // BLOCK)], axis=1)
    acc_out[...] = onward(acc_out) + jnp.dot(ups, hidden_ref[0], preferred_element_type=F32)
    product = lax.dot_general(
        lat_ref[0], gp_ref[...], (((0,), (0,)), ((), ())), preferred_element_type=F32
    )
    acc_in[...] = onward(acc_in) + product.reshape(acc_in.shape)

    @pl.when(step == last)
    def _():
        core = core_ref[0]
        share = jnp.sum(share_ref[...])
        high = share.astype(BF16).astype(F32)
        middle = (share - high).astype(BF16).astype(F32)
        low = share - high - middle
        column = lax.broadcasted_iota(jnp.int32, (channels, WIDE), 1) - (EXTRA + 3 * core)
        whole = jnp.concatenate([acc_out[...], jnp.zeros((WIDE - VPAD, channels), F32)], axis=0).T
        score = jnp.where(
            column == 0, high, jnp.where(column == 1, middle, jnp.where(column == 2, low, whole))
        )
        tail_ref[...] = score.reshape(tail_ref.shape)

        def group(g, carry):
            for half_ref, n in ((mine_ref, 2 * g + core), (other_ref, 2 * g + 1 - core)):
                half_ref[g, :, :channels] = acc_in[n].astype(BF16)
                half_ref[g, :, channels:] = tail_ref[n].astype(BF16)
            return carry

        lax.fori_loop(0, channels // 32, group, 0, unroll=4)


def backward(core, latent, hidden, slopes, upstream, w_out_t, share):
    members, points, channels = latent.shape
    steps = points // TILE
    per = TILE // BLOCK
    tile = pl.BlockSpec((1, TILE, channels), lambda i, c: (i // steps, i % steps, 0))
    half = (channels // 32, 16, channels + WIDE)
    grid_spec = pltpu.PrefetchScalarGridSpec(
        num_scalar_prefetch=1,
        grid=(members * steps,),
        in_specs=[
            tile,
            tile,
            tile,
            pl.BlockSpec((per, 1, VPAD, BLOCK), lambda i, c: (i % steps, i // steps, 0, 0)),
            pl.BlockSpec(w_out_t.shape, lambda i, c: (0, 0)),
            pl.BlockSpec((8, 128), lambda i, c: (0, 0)),
        ],
        out_specs=[pl.BlockSpec(memory_space=pltpu.VMEM)] * 2,
        scratch_shapes=[
            pltpu.VMEM((channels // 16, 16, channels), F32),
            pltpu.VMEM((VPAD, channels), F32),
            pltpu.VMEM((channels // 16, 16, WIDE), F32),
            pltpu.VMEM((WIDE, channels), BF16),
            pltpu.VMEM((TILE, channels), BF16),
        ],
    )
    return pl.pallas_call(
        backward_kernel,
        grid_spec=grid_spec,
        out_shape=[jax.ShapeDtypeStruct(half, BF16)] * 2,
        compiler_params=pltpu.CompilerParams(vmem_limit_bytes=BACKWARD_VMEM),
        name="backward",
    )(core, in_hbm(latent), in_hbm(hidden), in_hbm(slopes), upstream, in_hbm(w_out_t), share)


def latent_kernel(slope_ref, up_ref, wout_ref, win_ref, out_ref, wide_ref):
    @pl.when((pl.program_id(0) == 0) & (pl.program_id(1) == 0))
    def _():
        widen(wide_ref, wout_ref)

    for s in range(TILE // BLOCK):
        out_ref[0, pl.ds(s * BLOCK, BLOCK), :] = lax.dot_general(
            preact_grad(up_ref, slope_ref, wide_ref[...], s),
            win_ref[...],
            (((1,), (1,)), ((), ())),
            preferred_element_type=F32,
        ).astype(BF16)


def latent_grad(slopes, upstream, w_out_t, w_in):
    members, points, channels = slopes.shape
    per = TILE // BLOCK
    tile = pl.BlockSpec((1, TILE, channels), lambda m, i: (m, i, 0))
    return pl.pallas_call(
        latent_kernel,
        grid=(members, points // TILE),
        in_specs=[
            tile,
            pl.BlockSpec((per, 1, VPAD, BLOCK), lambda m, i: (i, m, 0, 0)),
            pl.BlockSpec(w_out_t.shape, lambda m, i: (0, 0)),
            pl.BlockSpec((channels, channels), lambda m, i: (0, 0)),
        ],
        out_specs=tile,
        out_shape=pltpu.HBM(slopes.shape, BF16),
        scratch_shapes=[pltpu.VMEM((WIDE, channels), BF16)],
        compiler_params=pltpu.CompilerParams(vmem_limit_bytes=LATENT_VMEM),
        cost_estimate=pl.CostEstimate(
            flops=2 * members * points * channels * (channels + WIDE),
            bytes_accessed=4 * members * points * channels,
            transcendentals=0,
        ),
        name="latent_grad",
    )(in_hbm(slopes), upstream, in_hbm(w_out_t), in_hbm(w_in))


def finish_kernel(grad_scale, loss_scale, pieces_ref, in_ref, out_ref, loss_ref):
    channels, variables = in_ref.shape[1], out_ref.shape[1]
    total = pieces_ref[0].astype(F32)
    for p in range(1, pieces_ref.shape[0]):
        total = total + pieces_ref[p].astype(F32)
    in_ref[...] = total[:, :channels] / grad_scale
    out_ref[...] = total[:, channels : channels + variables] / grad_scale
    tail = total[:1, channels:]
    column = lax.broadcasted_iota(jnp.int32, tail.shape, 1)
    loss_ref[0, 0] = jnp.sum(jnp.where(column >= EXTRA, tail, 0.0)) / loss_scale


def finish(pieces, variables, grad_scale, loss_scale):
    rows, wide = pieces.shape[1:]
    channels = wide - WIDE
    return pl.pallas_call(
        functools.partial(finish_kernel, grad_scale, loss_scale),
        out_specs=[
            pl.BlockSpec(memory_space=pltpu.VMEM),
            pl.BlockSpec(memory_space=pltpu.VMEM),
            pl.BlockSpec(memory_space=pltpu.SMEM),
        ],
        out_shape=[
            jax.ShapeDtypeStruct((rows, channels), F32),
            jax.ShapeDtypeStruct((rows, variables), F32),
            jax.ShapeDtypeStruct((1, 1), F32),
        ],
        compiler_params=pltpu.CompilerParams(vmem_limit_bytes=16 << 20),
        name="finish",
    )(pieces)


def exchange(x, axis, xor):
    size = lax.axis_size(axis)
    return lax.ppermute(x, axis, [(i, i ^ xor) for i in range(size)])


def body(latent, w_in, w_out, targets, area_units, var_weight):
    date_count, per, points, channels = latent.shape
    variables = w_out.shape[1]
    member_devices = lax.axis_size("xh") * lax.axis_size("z")
    members = per * member_devices
    npoints = points * lax.axis_size("y") * lax.axis_size("core")
    dates = date_count * lax.axis_size("dp")
    me = (lax.axis_index("xh") * lax.axis_size("z") + lax.axis_index("z")).astype(jnp.int32)
    core = lax.axis_index("core").astype(jnp.int32)

    area_total = jnp.sum(area_units.astype(F32))
    for axis, xor in (("core", 1), ("y", 1), ("y", 3)):
        area_total = area_total + exchange(area_total, axis, xor)
    scale = (npoints / area_total).reshape(1, 1)

    rows = latent.reshape(date_count * per, points, channels)
    w_out_t = w_out.T
    preact, pred = forward(rows, w_in, w_out_t)
    every = lax.all_to_all(pred, MEMBER, 0, 0, tiled=True)
    hidden, slopes = shape(preact)
    truth = jnp.pad(targets[0], ((0, VPAD - variables), (0, 0)))
    var_wide = jnp.broadcast_to(
        jnp.pad(var_weight, (0, VPAD - variables))[:, None], (VPAD, BLOCK)
    )
    area = area_units.reshape(points // BLOCK, 1, BLOCK)
    grad_pred, share = score(me.reshape(1), scale, every, truth, var_wide, area)
    upstream = lax.all_to_all(grad_pred, MEMBER, 0, 0, tiled=True)
    mine, other = backward(core.reshape(1), rows, hidden, slopes, upstream, w_out_t, share)
    wide = channels + WIDE
    both = (mine.astype(F32) + exchange(other, "core", 1).astype(F32)).astype(BF16)
    pieces = lax.all_to_all(both.reshape(-1, 8, wide), REST, 0, 0, tiled=True)
    grad_latent = latent_grad(slopes, upstream, w_out_t, w_in)
    grad_scale = math.sqrt(dates * members * npoints)
    grad_in, grad_out, loss = finish(pieces, variables, grad_scale, dates * npoints * variables)
    return loss.reshape(()), grad_latent.reshape(latent.shape), grad_in, grad_out


def solution(mesh):
    fine = Mesh(mesh.devices.reshape(2, 4, 4, 2, 2), ("xh", "z", "y", "core", "dp"))
    return jax.shard_map(
        body,
        mesh=fine,
        in_specs=(
            P("dp", MEMBER, ("y", "core"), None),
            P(),
            P(),
            P("dp", None, ("y", "core")),
            P(("y", "core")),
            P(),
        ),
        out_specs=(
            P(),
            P("dp", MEMBER, ("y", "core"), None),
            P(("xh", "z", "y", "core", "dp"), None),
            P(("xh", "z", "y", "core", "dp"), None),
        ),
        check_vma=False,
    )
```

```python
import functools
import math

import jax
import jax.numpy as jnp
from jax import lax
from jax.experimental import pallas as pl
from jax.experimental.pallas import tpu as pltpu
from jax.sharding import Mesh
from jax.sharding import PartitionSpec as P

GELU_C = 0.7978845608
GELU_A = 0.044715
SMOOTH = 0.01
BF16 = jnp.bfloat16
F32 = jnp.float32

BLOCK = 256
VPAD = 104
WIDE = 128
TILE = 1024
SUB = 256
EXTRA = 112

FORWARD_VMEM = 40 << 20
SCORE_VMEM = 16 << 20
BACKWARD_VMEM = 50 << 20
LATENT_VMEM = 40 << 20

MEMBER = ("xh", "z")
REST = ("xh", "z", "y", "dp")


def in_hbm(x):
    return pltpu.with_memory_space_constraint(x, pltpu.HBM)


def widen(wide_ref, wout_ref):
    variables = wout_ref.shape[0]
    wide_ref[...] = jnp.zeros_like(wide_ref)
    wide_ref[:variables, :] = wout_ref[...]


def forward_kernel(lat_ref, win_ref, wout_ref, hidden_ref, slope_ref, pred_ref, wide_ref):
    @pl.when((pl.program_id(0) == 0) & (pl.program_id(1) == 0))
    def _():
        widen(wide_ref, wout_ref)

    for s in range(TILE // SUB):
        rows = pl.ds(s * SUB, SUB)
        u = jnp.dot(lat_ref[0, rows, :], win_ref[...], preferred_element_type=F32).astype(BF16)
        u2 = u * u
        bent = jnp.tanh(u * (BF16(GELU_C) + BF16(GELU_C * GELU_A) * u2))
        half = BF16(0.5) + BF16(0.5) * bent
        hidden = u * half
        hidden_ref[0, rows, :] = hidden
        bend = BF16(GELU_C) + BF16(3.0 * GELU_A * GELU_C) * u2
        slope_ref[0, rows, :] = half + hidden * ((BF16(1.0) - bent) * bend)
        pred = lax.dot_general(
            hidden, wide_ref[...], (((1,), (1,)), ((), ())), preferred_element_type=F32
        )
        pred_ref[s, 0] = pred.T[:VPAD].astype(BF16)


def forward(latent, w_in, w_out_t):
    members, points, channels = latent.shape
    per = TILE // BLOCK
    tile = pl.BlockSpec((1, TILE, channels), lambda m, i: (m, i, 0))
    return pl.pallas_call(
        forward_kernel,
        grid=(members, points // TILE),
        in_specs=[
            tile,
            pl.BlockSpec((channels, channels), lambda m, i: (0, 0)),
            pl.BlockSpec(w_out_t.shape, lambda m, i: (0, 0)),
        ],
        out_specs=[
            tile,
            tile,
            pl.BlockSpec((per, 1, VPAD, BLOCK), lambda m, i: (i, m, 0, 0)),
        ],
        out_shape=[
            pltpu.HBM(latent.shape, BF16),
            pltpu.HBM(latent.shape, BF16),
            jax.ShapeDtypeStruct((points // BLOCK, members, VPAD, BLOCK), BF16),
        ],
        scratch_shapes=[pltpu.VMEM((WIDE, channels), BF16)],
        compiler_params=pltpu.CompilerParams(vmem_limit_bytes=FORWARD_VMEM),
        name="forward",
    )(in_hbm(latent), in_hbm(w_in), in_hbm(w_out_t))


def score_kernel(
    members, scale_ref, pred_ref, truth_ref, var_ref, area_ref, grad_ref, share_ref, held_ref, true_ref
):
    per = pred_ref.shape[1]
    scale = scale_ref[0, 0]
    self_phi = members * math.sqrt(SMOOTH) / (2.0 * (members - 1))
    true_ref[...] = truth_ref[...].astype(F32)
    for m in range(members):
        held_ref[m] = pred_ref[m // per, m % per].astype(F32)

    def part(rows, lanes):
        truth = true_ref[rows, lanes]
        x = [held_ref[m, rows, lanes] - truth for m in range(members)]
        weight = var_ref[rows, lanes] * (area_ref[0, :, lanes].astype(F32) * scale)
        grads = [None] * members
        roots = None
        for m in range(members - 1):
            for k in range(m + 1, members):
                d = x[m] - x[k]
                r = lax.rsqrt(d * d + SMOOTH)
                g = d * r
                roots = r if roots is None else roots + r
                grads[m] = g if grads[m] is None else grads[m] + g
                grads[k] = -g if grads[k] is None else grads[k] - g
        score = None
        for m in range(members):
            q = x[m] * x[m] + SMOOTH
            r = lax.rsqrt(q)
            spread = grads[m] * (1.0 / (members - 1))
            mine = q * r - x[m] * spread
            score = mine if score is None else score + mine
            held_ref[m, rows, lanes] = weight * (x[m] * r - spread)
        return weight * (score - roots * (SMOOTH / (members - 1)) - self_phi)

    def rows8(step, total):
        rows = pl.ds(pl.multiple_of(step * 8, 8), 8)
        for lane in range(BLOCK // 128):
            total = total + part(rows, pl.ds(lane * 128, 128))
        return total

    share_ref[...] = lax.fori_loop(0, VPAD // 8, rows8, jnp.zeros((8, 128), F32))
    for m in range(members):
        grad_ref[m // per, m % per] = held_ref[m].astype(BF16)


def score(me, scale, every, truth, var_weight, area):
    devices, per = every.shape[:2]
    members = devices * per
    vmem = pl.BlockSpec(memory_space=pltpu.VMEM)
    grid_spec = pltpu.PrefetchScalarGridSpec(
        num_scalar_prefetch=1,
        grid=(1,),
        in_specs=[
            pl.BlockSpec(memory_space=pltpu.SMEM),
            vmem,
            pl.BlockSpec((VPAD, BLOCK), lambda i, me: (0, me[0])),
            vmem,
            pl.BlockSpec((1, 1, BLOCK), lambda i, me: (me[0], 0, 0)),
        ],
        out_specs=[vmem, vmem],
        scratch_shapes=[
            pltpu.VMEM((members, VPAD, BLOCK), F32),
            pltpu.VMEM((VPAD, BLOCK), F32),
        ],
    )

    def kernel(me_ref, *refs):
        score_kernel(members, *refs)

    return pl.pallas_call(
        kernel,
        grid_spec=grid_spec,
        out_shape=[
            jax.ShapeDtypeStruct(every.shape, BF16),
            jax.ShapeDtypeStruct((8, 128), F32),
        ],
        compiler_params=pltpu.CompilerParams(vmem_limit_bytes=SCORE_VMEM),
        name="score",
    )(me, scale, every, truth, var_weight, area)


def preact_grad(up_ref, slope_ref, wide, s):
    block = jnp.concatenate(
        [up_ref[s, 0].astype(F32), jnp.zeros((WIDE - VPAD, BLOCK), F32)], axis=0
    )
    grad_hidden = jnp.dot(block.T.astype(BF16), wide, preferred_element_type=F32)
    return grad_hidden.astype(BF16) * slope_ref[0, pl.ds(s * BLOCK, BLOCK), :]


def backward_kernel(
    core_ref, lat_ref, hidden_ref, slope_ref, up_ref, wout_ref, share_ref,
    mine_ref, other_ref, acc_in, acc_out, tail_ref, wide_ref, gp_ref,
):
    step, last = pl.program_id(0), pl.num_programs(0) - 1
    channels = lat_ref.shape[2]

    @pl.when(step == 0)
    def _():
        widen(wide_ref, wout_ref)

    def onward(acc):
        return jnp.where(step == 0, 0.0, acc[...])

    for s in range(TILE // BLOCK):
        gp_ref[pl.ds(s * BLOCK, BLOCK), :] = preact_grad(up_ref, slope_ref, wide_ref[...], s)
    ups = jnp.concatenate([up_ref[s, 0] for s in range(TILE // BLOCK)], axis=1)
    acc_out[...] = onward(acc_out) + jnp.dot(ups, hidden_ref[0], preferred_element_type=F32)
    product = lax.dot_general(
        lat_ref[0], gp_ref[...], (((0,), (0,)), ((), ())), preferred_element_type=F32
    )
    acc_in[...] = onward(acc_in) + product.reshape(acc_in.shape)

    @pl.when(step == last)
    def _():
        core = core_ref[0]
        share = jnp.sum(share_ref[...])
        high = share.astype(BF16).astype(F32)
        middle = (share - high).astype(BF16).astype(F32)
        low = share - high - middle
        column = lax.broadcasted_iota(jnp.int32, (channels, WIDE), 1) - (EXTRA + 3 * core)
        whole = jnp.concatenate([acc_out[...], jnp.zeros((WIDE - VPAD, channels), F32)], axis=0).T
        score = jnp.where(
            column == 0, high, jnp.where(column == 1, middle, jnp.where(column == 2, low, whole))
        )
        tail_ref[...] = score.reshape(tail_ref.shape)

        def group(g, carry):
            for half_ref, n in ((mine_ref, 2 * g + core), (other_ref, 2 * g + 1 - core)):
                half_ref[g, :, :channels] = acc_in[n].astype(BF16)
                half_ref[g, :, channels:] = tail_ref[n].astype(BF16)
            return carry

        lax.fori_loop(0, channels // 32, group, 0, unroll=4)


def backward(core, latent, hidden, slopes, upstream, w_out_t, share):
    members, points, channels = latent.shape
    steps = points // TILE
    per = TILE // BLOCK
    tile = pl.BlockSpec((1, TILE, channels), lambda i, c: (i // steps, i % steps, 0))
    half = (channels // 32, 16, channels + WIDE)
    grid_spec = pltpu.PrefetchScalarGridSpec(
        num_scalar_prefetch=1,
        grid=(members * steps,),
        in_specs=[
            tile,
            tile,
            tile,
            pl.BlockSpec((per, 1, VPAD, BLOCK), lambda i, c: (i % steps, i // steps, 0, 0)),
            pl.BlockSpec(w_out_t.shape, lambda i, c: (0, 0)),
            pl.BlockSpec((8, 128), lambda i, c: (0, 0)),
        ],
        out_specs=[pl.BlockSpec(memory_space=pltpu.VMEM)] * 2,
        scratch_shapes=[
            pltpu.VMEM((channels // 16, 16, channels), F32),
            pltpu.VMEM((VPAD, channels), F32),
            pltpu.VMEM((channels // 16, 16, WIDE), F32),
            pltpu.VMEM((WIDE, channels), BF16),
            pltpu.VMEM((TILE, channels), BF16),
        ],
    )
    return pl.pallas_call(
        backward_kernel,
        grid_spec=grid_spec,
        out_shape=[jax.ShapeDtypeStruct(half, BF16)] * 2,
        compiler_params=pltpu.CompilerParams(vmem_limit_bytes=BACKWARD_VMEM),
        name="backward",
    )(core, in_hbm(latent), in_hbm(hidden), in_hbm(slopes), upstream, in_hbm(w_out_t), share)


def latent_kernel(slope_ref, up_ref, wout_ref, win_ref, out_ref, wide_ref):
    @pl.when((pl.program_id(0) == 0) & (pl.program_id(1) == 0))
    def _():
        widen(wide_ref, wout_ref)

    for s in range(TILE // BLOCK):
        out_ref[0, pl.ds(s * BLOCK, BLOCK), :] = lax.dot_general(
            preact_grad(up_ref, slope_ref, wide_ref[...], s),
            win_ref[...],
            (((1,), (1,)), ((), ())),
            preferred_element_type=F32,
        ).astype(BF16)


def latent_grad(slopes, upstream, w_out_t, w_in):
    members, points, channels = slopes.shape
    per = TILE // BLOCK
    tile = pl.BlockSpec((1, TILE, channels), lambda m, i: (m, i, 0))
    return pl.pallas_call(
        latent_kernel,
        grid=(members, points // TILE),
        in_specs=[
            tile,
            pl.BlockSpec((per, 1, VPAD, BLOCK), lambda m, i: (i, m, 0, 0)),
            pl.BlockSpec(w_out_t.shape, lambda m, i: (0, 0)),
            pl.BlockSpec((channels, channels), lambda m, i: (0, 0)),
        ],
        out_specs=tile,
        out_shape=pltpu.HBM(slopes.shape, BF16),
        scratch_shapes=[pltpu.VMEM((WIDE, channels), BF16)],
        compiler_params=pltpu.CompilerParams(vmem_limit_bytes=LATENT_VMEM),
        cost_estimate=pl.CostEstimate(
            flops=2 * members * points * channels * (channels + WIDE),
            bytes_accessed=4 * members * points * channels,
            transcendentals=0,
        ),
        name="latent_grad",
    )(in_hbm(slopes), upstream, in_hbm(w_out_t), in_hbm(w_in))


def finish_kernel(grad_scale, loss_scale, pieces_ref, in_ref, out_ref, loss_ref):
    channels, variables = in_ref.shape[1], out_ref.shape[1]
    total = pieces_ref[0].astype(F32)
    for p in range(1, pieces_ref.shape[0]):
        total = total + pieces_ref[p].astype(F32)
    in_ref[...] = total[:, :channels] / grad_scale
    out_ref[...] = total[:, channels : channels + variables] / grad_scale
    tail = total[:1, channels:]
    column = lax.broadcasted_iota(jnp.int32, tail.shape, 1)
    loss_ref[0, 0] = jnp.sum(jnp.where(column >= EXTRA, tail, 0.0)) / loss_scale


def finish(pieces, variables, grad_scale, loss_scale):
    rows, wide = pieces.shape[1:]
    channels = wide - WIDE
    return pl.pallas_call(
        functools.partial(finish_kernel, grad_scale, loss_scale),
        out_specs=[
            pl.BlockSpec(memory_space=pltpu.VMEM),
            pl.BlockSpec(memory_space=pltpu.VMEM),
            pl.BlockSpec(memory_space=pltpu.SMEM),
        ],
        out_shape=[
            jax.ShapeDtypeStruct((rows, channels), F32),
            jax.ShapeDtypeStruct((rows, variables), F32),
            jax.ShapeDtypeStruct((1, 1), F32),
        ],
        compiler_params=pltpu.CompilerParams(vmem_limit_bytes=16 << 20),
        name="finish",
    )(pieces)


def exchange(x, axis, xor):
    size = lax.axis_size(axis)
    return lax.ppermute(x, axis, [(i, i ^ xor) for i in range(size)])


def body(latent, w_in, w_out, targets, area_units, var_weight):
    date_count, per, points, channels = latent.shape
    variables = w_out.shape[1]
    member_devices = lax.axis_size("xh") * lax.axis_size("z")
    members = per * member_devices
    npoints = points * lax.axis_size("y") * lax.axis_size("core")
    dates = date_count * lax.axis_size("dp")
    me = (lax.axis_index("xh") * lax.axis_size("z") + lax.axis_index("z")).astype(jnp.int32)
    core = lax.axis_index("core").astype(jnp.int32)

    area_total = jnp.sum(area_units.astype(F32))
    for axis, xor in (("core", 1), ("y", 1), ("y", 3)):
        area_total = area_total + exchange(area_total, axis, xor)
    scale = (npoints / area_total).reshape(1, 1)

    rows = latent.reshape(date_count * per, points, channels)
    w_out_t = w_out.T
    hidden, slopes, pred = forward(rows, w_in, w_out_t)
    every = lax.all_to_all(pred, MEMBER, 0, 0, tiled=True)
    truth = jnp.pad(targets[0], ((0, VPAD - variables), (0, 0)))
    var_wide = jnp.broadcast_to(
        jnp.pad(var_weight, (0, VPAD - variables))[:, None], (VPAD, BLOCK)
    )
    area = area_units.reshape(points // BLOCK, 1, BLOCK)
    grad_pred, share = score(me.reshape(1), scale, every, truth, var_wide, area)
    upstream = lax.all_to_all(grad_pred, MEMBER, 0, 0, tiled=True)
    mine, other = backward(core.reshape(1), rows, hidden, slopes, upstream, w_out_t, share)
    wide = channels + WIDE
    both = (mine.astype(F32) + exchange(other, "core", 1).astype(F32)).astype(BF16)
    pieces = lax.all_to_all(both.reshape(-1, 8, wide), REST, 0, 0, tiled=True)
    grad_latent = latent_grad(slopes, upstream, w_out_t, w_in)
    grad_scale = math.sqrt(dates * members * npoints)
    grad_in, grad_out, loss = finish(pieces, variables, grad_scale, dates * npoints * variables)
    return loss.reshape(()), grad_latent.reshape(latent.shape), grad_in, grad_out


def solution(mesh):
    fine = Mesh(mesh.devices.reshape(2, 4, 4, 2, 2), ("xh", "z", "y", "core", "dp"))
    return jax.shard_map(
        body,
        mesh=fine,
        in_specs=(
            P("dp", MEMBER, ("y", "core"), None),
            P(),
            P(),
            P("dp", None, ("y", "core")),
            P(("y", "core")),
            P(),
        ),
        out_specs=(
            P(),
            P("dp", MEMBER, ("y", "core"), None),
            P(("xh", "z", "y", "core", "dp"), None),
            P(("xh", "z", "y", "core", "dp"), None),
        ),
        check_vma=False,
    )
```

```python
import functools
import math

import jax
import jax.numpy as jnp
from jax import lax
from jax.experimental import pallas as pl
from jax.experimental.pallas import tpu as pltpu
from jax.sharding import Mesh
from jax.sharding import PartitionSpec as P

GELU_C = 0.7978845608
GELU_A = 0.044715
SMOOTH = 0.01
BF16 = jnp.bfloat16
F32 = jnp.float32

BLOCK = 256
VPAD = 104
WIDE = 128
TILE = 1024
SUB = 256
EXTRA = 112

FORWARD_VMEM = 40 << 20
SCORE_VMEM = 16 << 20
BACKWARD_VMEM = 50 << 20
LATENT_VMEM = 40 << 20

MEMBER = ("xh", "z")
REST = ("xh", "z", "y", "dp")


def in_hbm(x):
    return pltpu.with_memory_space_constraint(x, pltpu.HBM)


def widen(wide_ref, wout_ref):
    variables = wout_ref.shape[0]
    wide_ref[...] = jnp.zeros_like(wide_ref)
    wide_ref[:variables, :] = wout_ref[...]


def forward_kernel(
    lat_ref, win_ref, wout_ref, area_ref, hidden_ref, slope_ref, pred_ref, total_ref, wide_ref
):
    @pl.when((pl.program_id(0) == 0) & (pl.program_id(1) == 0))
    def _():
        widen(wide_ref, wout_ref)
        total_ref[0, 0] = jnp.sum(area_ref[...].astype(F32))

    for s in range(TILE // SUB):
        rows = pl.ds(s * SUB, SUB)
        u = jnp.dot(lat_ref[0, rows, :], win_ref[...], preferred_element_type=F32).astype(BF16)
        u2 = u * u
        bent = jnp.tanh(u * (BF16(GELU_C) + BF16(GELU_C * GELU_A) * u2))
        half = BF16(0.5) + BF16(0.5) * bent
        hidden = u * half
        hidden_ref[0, rows, :] = hidden
        bend = BF16(GELU_C) + BF16(3.0 * GELU_A * GELU_C) * u2
        slope_ref[0, rows, :] = half + hidden * ((BF16(1.0) - bent) * bend)
        pred = lax.dot_general(
            hidden, wide_ref[...], (((1,), (1,)), ((), ())), preferred_element_type=F32
        )
        pred_ref[s, 0] = pred.T[:VPAD].astype(BF16)


def forward(latent, w_in, w_out_t, area):
    members, points, channels = latent.shape
    per = TILE // BLOCK
    tile = pl.BlockSpec((1, TILE, channels), lambda m, i: (m, i, 0))
    return pl.pallas_call(
        forward_kernel,
        grid=(members, points // TILE),
        in_specs=[
            tile,
            pl.BlockSpec((channels, channels), lambda m, i: (0, 0)),
            pl.BlockSpec(w_out_t.shape, lambda m, i: (0, 0)),
            pl.BlockSpec(area.shape, lambda m, i: (0, 0, 0)),
        ],
        out_specs=[
            tile,
            tile,
            pl.BlockSpec((per, 1, VPAD, BLOCK), lambda m, i: (i, m, 0, 0)),
            pl.BlockSpec(memory_space=pltpu.SMEM),
        ],
        out_shape=[
            pltpu.HBM(latent.shape, BF16),
            pltpu.HBM(latent.shape, BF16),
            jax.ShapeDtypeStruct((points // BLOCK, members, VPAD, BLOCK), BF16),
            jax.ShapeDtypeStruct((1, 1), F32),
        ],
        scratch_shapes=[pltpu.VMEM((WIDE, channels), BF16)],
        compiler_params=pltpu.CompilerParams(vmem_limit_bytes=FORWARD_VMEM),
        name="forward",
    )(in_hbm(latent), in_hbm(w_in), in_hbm(w_out_t), area)


def score_kernel(
    members, scale_ref, pred_ref, truth_ref, var_ref, area_ref, grad_ref, share_ref,
    held_ref, true_ref, each_ref,
):
    per = pred_ref.shape[1]
    scale = scale_ref[0, 0]
    self_phi = members * math.sqrt(SMOOTH) / (2.0 * (members - 1))
    variables = truth_ref.shape[0]
    true_ref[...] = jnp.zeros_like(true_ref)
    true_ref[:variables, :] = truth_ref[...].astype(F32)
    each_ref[...] = jnp.broadcast_to(var_ref[...], (WIDE, WIDE)).T[:VPAD]
    for m in range(members):
        held_ref[m] = pred_ref[m // per, m % per].astype(F32)

    def part(rows, lanes):
        truth = true_ref[rows, lanes]
        x = [held_ref[m, rows, lanes] - truth for m in range(members)]
        weight = each_ref[rows, :] * (area_ref[0, :, lanes].astype(F32) * scale)
        grads = [None] * members
        roots = None
        for m in range(members - 1):
            for k in range(m + 1, members):
                d = x[m] - x[k]
                r = lax.rsqrt(d * d + SMOOTH)
                g = d * r
                roots = r if roots is None else roots + r
                grads[m] = g if grads[m] is None else grads[m] + g
                grads[k] = -g if grads[k] is None else grads[k] - g
        score = None
        for m in range(members):
            q = x[m] * x[m] + SMOOTH
            r = lax.rsqrt(q)
            spread = grads[m] * (1.0 / (members - 1))
            mine = q * r - x[m] * spread
            score = mine if score is None else score + mine
            held_ref[m, rows, lanes] = weight * (x[m] * r - spread)
        return weight * (score - roots * (SMOOTH / (members - 1)) - self_phi)

    def rows8(step, total):
        rows = pl.ds(pl.multiple_of(step * 8, 8), 8)
        for lane in range(BLOCK // 128):
            total = total + part(rows, pl.ds(lane * 128, 128))
        return total

    share_ref[...] = lax.fori_loop(0, VPAD // 8, rows8, jnp.zeros((8, 128), F32))
    for m in range(members):
        grad_ref[m // per, m % per] = held_ref[m].astype(BF16)


def score(me, scale, every, truth, var_weight, area):
    devices, per = every.shape[:2]
    members = devices * per
    vmem = pl.BlockSpec(memory_space=pltpu.VMEM)
    grid_spec = pltpu.PrefetchScalarGridSpec(
        num_scalar_prefetch=1,
        grid=(1,),
        in_specs=[
            pl.BlockSpec(memory_space=pltpu.SMEM),
            vmem,
            pl.BlockSpec((truth.shape[0], BLOCK), lambda i, me: (0, me[0])),
            vmem,
            pl.BlockSpec((1, 1, BLOCK), lambda i, me: (me[0], 0, 0)),
        ],
        out_specs=[vmem, vmem],
        scratch_shapes=[
            pltpu.VMEM((members, VPAD, BLOCK), F32),
            pltpu.VMEM((VPAD, BLOCK), F32),
            pltpu.VMEM((VPAD, WIDE), F32),
        ],
    )

    def kernel(me_ref, *refs):
        score_kernel(members, *refs)

    return pl.pallas_call(
        kernel,
        grid_spec=grid_spec,
        out_shape=[
            jax.ShapeDtypeStruct(every.shape, BF16),
            jax.ShapeDtypeStruct((8, 128), F32),
        ],
        compiler_params=pltpu.CompilerParams(vmem_limit_bytes=SCORE_VMEM),
        name="score",
    )(me, scale, every, truth, var_weight, area)


def preact_grad(up_ref, slope_ref, wide, s):
    block = jnp.concatenate(
        [up_ref[s, 0].astype(F32), jnp.zeros((WIDE - VPAD, BLOCK), F32)], axis=0
    )
    grad_hidden = jnp.dot(block.T.astype(BF16), wide, preferred_element_type=F32)
    return grad_hidden.astype(BF16) * slope_ref[0, pl.ds(s * BLOCK, BLOCK), :]


def backward_kernel(
    core_ref, lat_ref, hidden_ref, slope_ref, up_ref, wout_ref, share_ref,
    mine_ref, other_ref, acc_in, acc_out, tail_ref, wide_ref, gp_ref,
):
    step, last = pl.program_id(0), pl.num_programs(0) - 1
    channels = lat_ref.shape[2]

    @pl.when(step == 0)
    def _():
        widen(wide_ref, wout_ref)

    def onward(acc):
        return jnp.where(step == 0, 0.0, acc[...])

    for s in range(TILE // BLOCK):
        gp_ref[pl.ds(s * BLOCK, BLOCK), :] = preact_grad(up_ref, slope_ref, wide_ref[...], s)
    ups = jnp.concatenate([up_ref[s, 0] for s in range(TILE // BLOCK)], axis=1)
    acc_out[...] = onward(acc_out) + jnp.dot(ups, hidden_ref[0], preferred_element_type=F32)
    product = lax.dot_general(
        lat_ref[0], gp_ref[...], (((0,), (0,)), ((), ())), preferred_element_type=F32
    )
    acc_in[...] = onward(acc_in) + product.reshape(acc_in.shape)

    @pl.when(step == last)
    def _():
        core = core_ref[0]
        share = jnp.sum(share_ref[...])
        high = share.astype(BF16).astype(F32)
        middle = (share - high).astype(BF16).astype(F32)
        low = share - high - middle
        column = lax.broadcasted_iota(jnp.int32, (channels, WIDE), 1) - (EXTRA + 3 * core)
        whole = jnp.concatenate([acc_out[...], jnp.zeros((WIDE - VPAD, channels), F32)], axis=0).T
        score = jnp.where(
            column == 0, high, jnp.where(column == 1, middle, jnp.where(column == 2, low, whole))
        )
        tail_ref[...] = score.reshape(tail_ref.shape)

        def group(g, carry):
            for half_ref, n in ((mine_ref, 2 * g + core), (other_ref, 2 * g + 1 - core)):
                half_ref[g, :, :channels] = acc_in[n].astype(BF16)
                half_ref[g, :, channels:] = tail_ref[n].astype(BF16)
            return carry

        lax.fori_loop(0, channels // 32, group, 0, unroll=4)


def backward(core, latent, hidden, slopes, upstream, w_out_t, share):
    members, points, channels = latent.shape
    steps = points // TILE
    per = TILE // BLOCK
    tile = pl.BlockSpec((1, TILE, channels), lambda i, c: (i // steps, i % steps, 0))
    half = (channels // 32, 16, channels + WIDE)
    grid_spec = pltpu.PrefetchScalarGridSpec(
        num_scalar_prefetch=1,
        grid=(members * steps,),
        in_specs=[
            tile,
            tile,
            tile,
            pl.BlockSpec((per, 1, VPAD, BLOCK), lambda i, c: (i % steps, i // steps, 0, 0)),
            pl.BlockSpec(w_out_t.shape, lambda i, c: (0, 0)),
            pl.BlockSpec((8, 128), lambda i, c: (0, 0)),
        ],
        out_specs=[pl.BlockSpec(memory_space=pltpu.VMEM)] * 2,
        scratch_shapes=[
            pltpu.VMEM((channels // 16, 16, channels), F32),
            pltpu.VMEM((VPAD, channels), F32),
            pltpu.VMEM((channels // 16, 16, WIDE), F32),
            pltpu.VMEM((WIDE, channels), BF16),
            pltpu.VMEM((TILE, channels), BF16),
        ],
    )
    return pl.pallas_call(
        backward_kernel,
        grid_spec=grid_spec,
        out_shape=[jax.ShapeDtypeStruct(half, BF16)] * 2,
        compiler_params=pltpu.CompilerParams(vmem_limit_bytes=BACKWARD_VMEM),
        name="backward",
    )(core, in_hbm(latent), in_hbm(hidden), in_hbm(slopes), upstream, in_hbm(w_out_t), share)


def latent_kernel(slope_ref, up_ref, wout_ref, win_ref, out_ref, wide_ref):
    @pl.when((pl.program_id(0) == 0) & (pl.program_id(1) == 0))
    def _():
        widen(wide_ref, wout_ref)

    for s in range(TILE // BLOCK):
        out_ref[0, pl.ds(s * BLOCK, BLOCK), :] = lax.dot_general(
            preact_grad(up_ref, slope_ref, wide_ref[...], s),
            win_ref[...],
            (((1,), (1,)), ((), ())),
            preferred_element_type=F32,
        ).astype(BF16)


def latent_grad(slopes, upstream, w_out_t, w_in):
    members, points, channels = slopes.shape
    per = TILE // BLOCK
    tile = pl.BlockSpec((1, TILE, channels), lambda m, i: (m, i, 0))
    return pl.pallas_call(
        latent_kernel,
        grid=(members, points // TILE),
        in_specs=[
            tile,
            pl.BlockSpec((per, 1, VPAD, BLOCK), lambda m, i: (i, m, 0, 0)),
            pl.BlockSpec(w_out_t.shape, lambda m, i: (0, 0)),
            pl.BlockSpec((channels, channels), lambda m, i: (0, 0)),
        ],
        out_specs=tile,
        out_shape=pltpu.HBM(slopes.shape, BF16),
        scratch_shapes=[pltpu.VMEM((WIDE, channels), BF16)],
        compiler_params=pltpu.CompilerParams(vmem_limit_bytes=LATENT_VMEM),
        cost_estimate=pl.CostEstimate(
            flops=2 * members * points * channels * (channels + WIDE),
            bytes_accessed=4 * members * points * channels,
            transcendentals=0,
        ),
        name="latent_grad",
    )(in_hbm(slopes), upstream, in_hbm(w_out_t), in_hbm(w_in))


def finish_kernel(grad_scale, loss_scale, pieces_ref, in_ref, out_ref, loss_ref):
    channels, variables = in_ref.shape[1], out_ref.shape[1]
    total = pieces_ref[0].astype(F32)
    for p in range(1, pieces_ref.shape[0]):
        total = total + pieces_ref[p].astype(F32)
    in_ref[...] = total[:, :channels] / grad_scale
    out_ref[...] = total[:, channels : channels + variables] / grad_scale
    tail = total[:1, channels:]
    column = lax.broadcasted_iota(jnp.int32, tail.shape, 1)
    loss_ref[0, 0] = jnp.sum(jnp.where(column >= EXTRA, tail, 0.0)) / loss_scale


def finish(pieces, variables, grad_scale, loss_scale):
    rows, wide = pieces.shape[1:]
    channels = wide - WIDE
    return pl.pallas_call(
        functools.partial(finish_kernel, grad_scale, loss_scale),
        out_specs=[
            pl.BlockSpec(memory_space=pltpu.VMEM),
            pl.BlockSpec(memory_space=pltpu.VMEM),
            pl.BlockSpec(memory_space=pltpu.SMEM),
        ],
        out_shape=[
            jax.ShapeDtypeStruct((rows, channels), F32),
            jax.ShapeDtypeStruct((rows, variables), F32),
            jax.ShapeDtypeStruct((1, 1), F32),
        ],
        compiler_params=pltpu.CompilerParams(vmem_limit_bytes=16 << 20),
        name="finish",
    )(pieces)


def exchange(x, axis, xor):
    size = lax.axis_size(axis)
    return lax.ppermute(x, axis, [(i, i ^ xor) for i in range(size)])


def body(latent, w_in, w_out, targets, area_units, var_weight):
    date_count, per, points, channels = latent.shape
    variables = w_out.shape[1]
    member_devices = lax.axis_size("xh") * lax.axis_size("z")
    members = per * member_devices
    npoints = points * lax.axis_size("y") * lax.axis_size("core")
    dates = date_count * lax.axis_size("dp")
    me = (lax.axis_index("xh") * lax.axis_size("z") + lax.axis_index("z")).astype(jnp.int32)
    core = lax.axis_index("core").astype(jnp.int32)

    rows = latent.reshape(date_count * per, points, channels)
    w_out_t = w_out.T
    area = area_units.reshape(points // BLOCK, 1, BLOCK)
    hidden, slopes, pred, area_total = forward(rows, w_in, w_out_t, area)
    for axis, xor in (("core", 1), ("y", 1), ("y", 3)):
        area_total = area_total + exchange(area_total, axis, xor)
    scale = npoints / area_total
    every = lax.all_to_all(pred, MEMBER, 0, 0, tiled=True)
    var_row = jnp.pad(var_weight, (0, WIDE - variables)).reshape(1, WIDE)
    grad_pred, share = score(me.reshape(1), scale, every, targets[0], var_row, area)
    upstream = lax.all_to_all(grad_pred, MEMBER, 0, 0, tiled=True)
    mine, other = backward(core.reshape(1), rows, hidden, slopes, upstream, w_out_t, share)
    wide = channels + WIDE
    both = (mine.astype(F32) + exchange(other, "core", 1).astype(F32)).astype(BF16)
    pieces = lax.all_to_all(both.reshape(-1, 8, wide), REST, 0, 0, tiled=True)
    grad_latent = latent_grad(slopes, upstream, w_out_t, w_in)
    grad_scale = math.sqrt(dates * members * npoints)
    grad_in, grad_out, loss = finish(pieces, variables, grad_scale, dates * npoints * variables)
    return loss.reshape(()), grad_latent.reshape(latent.shape), grad_in, grad_out


def solution(mesh):
    fine = Mesh(mesh.devices.reshape(2, 4, 4, 2, 2), ("xh", "z", "y", "core", "dp"))
    return jax.shard_map(
        body,
        mesh=fine,
        in_specs=(
            P("dp", MEMBER, ("y", "core"), None),
            P(),
            P(),
            P("dp", None, ("y", "core")),
            P(("y", "core")),
            P(),
        ),
        out_specs=(
            P(),
            P("dp", MEMBER, ("y", "core"), None),
            P(("xh", "z", "y", "core", "dp"), None),
            P(("xh", "z", "y", "core", "dp"), None),
        ),
        check_vma=False,
    )
```

```python
import functools
import math

import jax
import jax.numpy as jnp
from jax import lax
from jax.experimental import pallas as pl
from jax.experimental.pallas import tpu as pltpu
from jax.sharding import Mesh
from jax.sharding import PartitionSpec as P

GELU_C = 0.7978845608
GELU_A = 0.044715
SMOOTH = 0.01
BF16 = jnp.bfloat16
F32 = jnp.float32

BLOCK = 256
VPAD = 104
WIDE = 128
TILE = 1024
SUB = 256
EXTRA = 112

FORWARD_VMEM = 40 << 20
SCORE_VMEM = 16 << 20
BACKWARD_VMEM = 50 << 20
LATENT_VMEM = 40 << 20

MEMBER = ("xh", "z")
REST = ("xh", "z", "y", "dp")


def in_hbm(x):
    return pltpu.with_memory_space_constraint(x, pltpu.HBM)


def widen(wide_ref, wout_ref):
    variables = wout_ref.shape[0]
    wide_ref[...] = jnp.zeros_like(wide_ref)
    wide_ref[:variables, :] = wout_ref[...]


def forward_kernel(
    lat_ref, win_ref, wout_ref, area_ref, hidden_ref, slope_ref, pred_ref, total_ref, wide_ref
):
    @pl.when((pl.program_id(0) == 0) & (pl.program_id(1) == 0))
    def _():
        widen(wide_ref, wout_ref)
        total_ref[0, 0] = jnp.sum(area_ref[...].astype(F32))

    for s in range(TILE // SUB):
        rows = pl.ds(s * SUB, SUB)
        u = jnp.dot(lat_ref[0, rows, :], win_ref[...], preferred_element_type=F32).astype(BF16)
        u2 = u * u
        bent = jnp.tanh(u * (BF16(GELU_C) + BF16(GELU_C * GELU_A) * u2))
        half = BF16(0.5) + BF16(0.5) * bent
        hidden = u * half
        hidden_ref[0, rows, :] = hidden
        bend = BF16(GELU_C) + BF16(3.0 * GELU_A * GELU_C) * u2
        slope_ref[0, rows, :] = half + hidden * ((BF16(1.0) - bent) * bend)
        pred = lax.dot_general(
            hidden, wide_ref[...], (((1,), (1,)), ((), ())), preferred_element_type=F32
        )
        pred_ref[s, 0] = pred.T[:VPAD].astype(BF16)


def forward(latent, w_in, w_out_t, area):
    members, points, channels = latent.shape
    per = TILE // BLOCK
    tile = pl.BlockSpec((1, TILE, channels), lambda m, i: (m, i, 0))
    return pl.pallas_call(
        forward_kernel,
        grid=(members, points // TILE),
        in_specs=[
            tile,
            pl.BlockSpec((channels, channels), lambda m, i: (0, 0)),
            pl.BlockSpec(w_out_t.shape, lambda m, i: (0, 0)),
            pl.BlockSpec(area.shape, lambda m, i: (0, 0, 0)),
        ],
        out_specs=[
            tile,
            tile,
            pl.BlockSpec((per, 1, VPAD, BLOCK), lambda m, i: (i, m, 0, 0)),
            pl.BlockSpec(memory_space=pltpu.SMEM),
        ],
        out_shape=[
            pltpu.HBM(latent.shape, BF16),
            pltpu.HBM(latent.shape, BF16),
            jax.ShapeDtypeStruct((points // BLOCK, members, VPAD, BLOCK), BF16),
            jax.ShapeDtypeStruct((1, 1), F32),
        ],
        scratch_shapes=[pltpu.VMEM((WIDE, channels), BF16)],
        compiler_params=pltpu.CompilerParams(vmem_limit_bytes=FORWARD_VMEM),
        name="forward",
    )(in_hbm(latent), in_hbm(w_in), in_hbm(w_out_t), area)


def score_kernel(
    members, scale_ref, pred_ref, truth_ref, var_ref, area_ref, grad_ref, share_ref,
    held_ref, true_ref, each_ref,
):
    per = pred_ref.shape[1]
    scale = scale_ref[0, 0]
    self_phi = members * math.sqrt(SMOOTH) / (2.0 * (members - 1))
    variables = truth_ref.shape[0]
    true_ref[...] = jnp.zeros_like(true_ref)
    true_ref[:variables, :] = truth_ref[...].astype(F32)
    each_ref[...] = jnp.zeros_like(each_ref)
    each_ref[:variables, :] = jnp.broadcast_to(var_ref[...], (WIDE, variables)).T
    for m in range(members):
        held_ref[m] = pred_ref[m // per, m % per].astype(F32)

    def part(rows, lanes):
        truth = true_ref[rows, lanes]
        x = [held_ref[m, rows, lanes] - truth for m in range(members)]
        weight = each_ref[rows, :] * (area_ref[0, :, lanes].astype(F32) * scale)
        grads = [None] * members
        roots = None
        for m in range(members - 1):
            for k in range(m + 1, members):
                d = x[m] - x[k]
                r = lax.rsqrt(d * d + SMOOTH)
                g = d * r
                roots = r if roots is None else roots + r
                grads[m] = g if grads[m] is None else grads[m] + g
                grads[k] = -g if grads[k] is None else grads[k] - g
        score = None
        for m in range(members):
            q = x[m] * x[m] + SMOOTH
            r = lax.rsqrt(q)
            spread = grads[m] * (1.0 / (members - 1))
            mine = q * r - x[m] * spread
            score = mine if score is None else score + mine
            held_ref[m, rows, lanes] = weight * (x[m] * r - spread)
        return weight * (score - roots * (SMOOTH / (members - 1)) - self_phi)

    def rows8(step, total):
        rows = pl.ds(pl.multiple_of(step * 8, 8), 8)
        for lane in range(BLOCK // 128):
            total = total + part(rows, pl.ds(lane * 128, 128))
        return total

    share_ref[...] = lax.fori_loop(0, VPAD // 8, rows8, jnp.zeros((8, 128), F32))
    for m in range(members):
        grad_ref[m // per, m % per] = held_ref[m].astype(BF16)


def score(me, scale, every, truth, var_weight, area):
    devices, per = every.shape[:2]
    members = devices * per
    vmem = pl.BlockSpec(memory_space=pltpu.VMEM)
    grid_spec = pltpu.PrefetchScalarGridSpec(
        num_scalar_prefetch=1,
        grid=(1,),
        in_specs=[
            pl.BlockSpec(memory_space=pltpu.SMEM),
            vmem,
            pl.BlockSpec((truth.shape[0], BLOCK), lambda i, me: (0, me[0])),
            vmem,
            pl.BlockSpec((1, 1, BLOCK), lambda i, me: (me[0], 0, 0)),
        ],
        out_specs=[vmem, vmem],
        scratch_shapes=[
            pltpu.VMEM((members, VPAD, BLOCK), F32),
            pltpu.VMEM((VPAD, BLOCK), F32),
            pltpu.VMEM((VPAD, WIDE), F32),
        ],
    )

    def kernel(me_ref, *refs):
        score_kernel(members, *refs)

    return pl.pallas_call(
        kernel,
        grid_spec=grid_spec,
        out_shape=[
            jax.ShapeDtypeStruct(every.shape, BF16),
            jax.ShapeDtypeStruct((8, 128), F32),
        ],
        compiler_params=pltpu.CompilerParams(vmem_limit_bytes=SCORE_VMEM),
        name="score",
    )(me, scale, every, truth, var_weight, area)


def preact_grad(up_ref, slope_ref, wide, s):
    block = jnp.concatenate(
        [up_ref[s, 0].astype(F32), jnp.zeros((WIDE - VPAD, BLOCK), F32)], axis=0
    )
    grad_hidden = jnp.dot(block.T.astype(BF16), wide, preferred_element_type=F32)
    return grad_hidden.astype(BF16) * slope_ref[0, pl.ds(s * BLOCK, BLOCK), :]


def backward_kernel(
    core_ref, lat_ref, hidden_ref, slope_ref, up_ref, wout_ref, share_ref,
    mine_ref, other_ref, acc_in, acc_out, tail_ref, wide_ref, gp_ref,
):
    step, last = pl.program_id(0), pl.num_programs(0) - 1
    channels = lat_ref.shape[2]

    @pl.when(step == 0)
    def _():
        widen(wide_ref, wout_ref)

    def onward(acc):
        return jnp.where(step == 0, 0.0, acc[...])

    for s in range(TILE // BLOCK):
        gp_ref[pl.ds(s * BLOCK, BLOCK), :] = preact_grad(up_ref, slope_ref, wide_ref[...], s)
    ups = jnp.concatenate([up_ref[s, 0] for s in range(TILE // BLOCK)], axis=1)
    acc_out[...] = onward(acc_out) + jnp.dot(ups, hidden_ref[0], preferred_element_type=F32)
    product = lax.dot_general(
        lat_ref[0], gp_ref[...], (((0,), (0,)), ((), ())), preferred_element_type=F32
    )
    acc_in[...] = onward(acc_in) + product.reshape(acc_in.shape)

    @pl.when(step == last)
    def _():
        core = core_ref[0]
        share = jnp.sum(share_ref[...])
        high = share.astype(BF16).astype(F32)
        middle = (share - high).astype(BF16).astype(F32)
        low = share - high - middle
        column = lax.broadcasted_iota(jnp.int32, (channels, WIDE), 1) - (EXTRA + 3 * core)
        whole = jnp.concatenate([acc_out[...], jnp.zeros((WIDE - VPAD, channels), F32)], axis=0).T
        score = jnp.where(
            column == 0, high, jnp.where(column == 1, middle, jnp.where(column == 2, low, whole))
        )
        tail_ref[...] = score.reshape(tail_ref.shape)

        def group(g, carry):
            for half_ref, n in ((mine_ref, 2 * g + core), (other_ref, 2 * g + 1 - core)):
                half_ref[g, :, :channels] = acc_in[n].astype(BF16)
                half_ref[g, :, channels:] = tail_ref[n].astype(BF16)
            return carry

        lax.fori_loop(0, channels // 32, group, 0, unroll=4)


def backward(core, latent, hidden, slopes, upstream, w_out_t, share):
    members, points, channels = latent.shape
    steps = points // TILE
    per = TILE // BLOCK
    tile = pl.BlockSpec((1, TILE, channels), lambda i, c: (i // steps, i % steps, 0))
    half = (channels // 32, 16, channels + WIDE)
    grid_spec = pltpu.PrefetchScalarGridSpec(
        num_scalar_prefetch=1,
        grid=(members * steps,),
        in_specs=[
            tile,
            tile,
            tile,
            pl.BlockSpec((per, 1, VPAD, BLOCK), lambda i, c: (i % steps, i // steps, 0, 0)),
            pl.BlockSpec(w_out_t.shape, lambda i, c: (0, 0)),
            pl.BlockSpec((8, 128), lambda i, c: (0, 0)),
        ],
        out_specs=[pl.BlockSpec(memory_space=pltpu.VMEM)] * 2,
        scratch_shapes=[
            pltpu.VMEM((channels // 16, 16, channels), F32),
            pltpu.VMEM((VPAD, channels), F32),
            pltpu.VMEM((channels // 16, 16, WIDE), F32),
            pltpu.VMEM((WIDE, channels), BF16),
            pltpu.VMEM((TILE, channels), BF16),
        ],
    )
    return pl.pallas_call(
        backward_kernel,
        grid_spec=grid_spec,
        out_shape=[jax.ShapeDtypeStruct(half, BF16)] * 2,
        compiler_params=pltpu.CompilerParams(vmem_limit_bytes=BACKWARD_VMEM),
        name="backward",
    )(core, in_hbm(latent), in_hbm(hidden), in_hbm(slopes), upstream, in_hbm(w_out_t), share)


def latent_kernel(slope_ref, up_ref, wout_ref, win_ref, out_ref, wide_ref):
    @pl.when((pl.program_id(0) == 0) & (pl.program_id(1) == 0))
    def _():
        widen(wide_ref, wout_ref)

    for s in range(TILE // BLOCK):
        out_ref[0, pl.ds(s * BLOCK, BLOCK), :] = lax.dot_general(
            preact_grad(up_ref, slope_ref, wide_ref[...], s),
            win_ref[...],
            (((1,), (1,)), ((), ())),
            preferred_element_type=F32,
        ).astype(BF16)


def latent_grad(slopes, upstream, w_out_t, w_in):
    members, points, channels = slopes.shape
    per = TILE // BLOCK
    tile = pl.BlockSpec((1, TILE, channels), lambda m, i: (m, i, 0))
    return pl.pallas_call(
        latent_kernel,
        grid=(members, points // TILE),
        in_specs=[
            tile,
            pl.BlockSpec((per, 1, VPAD, BLOCK), lambda m, i: (i, m, 0, 0)),
            pl.BlockSpec(w_out_t.shape, lambda m, i: (0, 0)),
            pl.BlockSpec((channels, channels), lambda m, i: (0, 0)),
        ],
        out_specs=tile,
        out_shape=pltpu.HBM(slopes.shape, BF16),
        scratch_shapes=[pltpu.VMEM((WIDE, channels), BF16)],
        compiler_params=pltpu.CompilerParams(vmem_limit_bytes=LATENT_VMEM),
        cost_estimate=pl.CostEstimate(
            flops=2 * members * points * channels * (channels + WIDE),
            bytes_accessed=4 * members * points * channels,
            transcendentals=0,
        ),
        name="latent_grad",
    )(in_hbm(slopes), upstream, in_hbm(w_out_t), in_hbm(w_in))


def finish_kernel(grad_scale, loss_scale, pieces_ref, in_ref, out_ref, loss_ref):
    channels, variables = in_ref.shape[1], out_ref.shape[1]
    total = pieces_ref[0].astype(F32)
    for p in range(1, pieces_ref.shape[0]):
        total = total + pieces_ref[p].astype(F32)
    in_ref[...] = total[:, :channels] / grad_scale
    out_ref[...] = total[:, channels : channels + variables] / grad_scale
    tail = total[:1, channels:]
    column = lax.broadcasted_iota(jnp.int32, tail.shape, 1)
    loss_ref[0, 0] = jnp.sum(jnp.where(column >= EXTRA, tail, 0.0)) / loss_scale


def finish(pieces, variables, grad_scale, loss_scale):
    rows, wide = pieces.shape[1:]
    channels = wide - WIDE
    return pl.pallas_call(
        functools.partial(finish_kernel, grad_scale, loss_scale),
        out_specs=[
            pl.BlockSpec(memory_space=pltpu.VMEM),
            pl.BlockSpec(memory_space=pltpu.VMEM),
            pl.BlockSpec(memory_space=pltpu.SMEM),
        ],
        out_shape=[
            jax.ShapeDtypeStruct((rows, channels), F32),
            jax.ShapeDtypeStruct((rows, variables), F32),
            jax.ShapeDtypeStruct((1, 1), F32),
        ],
        compiler_params=pltpu.CompilerParams(vmem_limit_bytes=16 << 20),
        name="finish",
    )(pieces)


def exchange(x, axis, xor):
    size = lax.axis_size(axis)
    return lax.ppermute(x, axis, [(i, i ^ xor) for i in range(size)])


def body(latent, w_in, w_out, targets, area_units, var_weight):
    date_count, per, points, channels = latent.shape
    variables = w_out.shape[1]
    member_devices = lax.axis_size("xh") * lax.axis_size("z")
    members = per * member_devices
    npoints = points * lax.axis_size("y") * lax.axis_size("core")
    dates = date_count * lax.axis_size("dp")
    me = (lax.axis_index("xh") * lax.axis_size("z") + lax.axis_index("z")).astype(jnp.int32)
    core = lax.axis_index("core").astype(jnp.int32)

    rows = latent.reshape(date_count * per, points, channels)
    w_out_t = w_out.T
    area = area_units.reshape(points // BLOCK, 1, BLOCK)
    hidden, slopes, pred, area_total = forward(rows, w_in, w_out_t, area)
    for axis, xor in (("core", 1), ("y", 1), ("y", 3)):
        area_total = area_total + exchange(area_total, axis, xor)
    scale = npoints / area_total
    every = lax.all_to_all(pred, MEMBER, 0, 0, tiled=True)
    var_row = var_weight.reshape(1, variables)
    grad_pred, share = score(me.reshape(1), scale, every, targets[0], var_row, area)
    upstream = lax.all_to_all(grad_pred, MEMBER, 0, 0, tiled=True)
    mine, other = backward(core.reshape(1), rows, hidden, slopes, upstream, w_out_t, share)
    wide = channels + WIDE
    both = (mine.astype(F32) + exchange(other, "core", 1).astype(F32)).astype(BF16)
    pieces = lax.all_to_all(both.reshape(-1, 8, wide), REST, 0, 0, tiled=True)
    grad_latent = latent_grad(slopes, upstream, w_out_t, w_in)
    grad_scale = math.sqrt(dates * members * npoints)
    grad_in, grad_out, loss = finish(pieces, variables, grad_scale, dates * npoints * variables)
    return loss.reshape(()), grad_latent.reshape(latent.shape), grad_in, grad_out


def solution(mesh):
    fine = Mesh(mesh.devices.reshape(2, 4, 4, 2, 2), ("xh", "z", "y", "core", "dp"))
    return jax.shard_map(
        body,
        mesh=fine,
        in_specs=(
            P("dp", MEMBER, ("y", "core"), None),
            P(),
            P(),
            P("dp", None, ("y", "core")),
            P(("y", "core")),
            P(),
        ),
        out_specs=(
            P(),
            P("dp", MEMBER, ("y", "core"), None),
            P(("xh", "z", "y", "core", "dp"), None),
            P(("xh", "z", "y", "core", "dp"), None),
        ),
        check_vma=False,
    )
```
